512 devices in a mesh: gx: 32 (over y, z_hi, x), gy: 16 (over z_lo, core).
Axes of the slice: x: 4, y: 4, z: 16 (z_hi: 2, z_lo: 8; z = z_hi * 8 + z_lo), core: 2. Of those that a mesh axis runs over, the one named last changes fastest.
Arguments:
- e_field: float32 [3, 256, 256, 128], P(None, 'gx', 'gy'), may hold values from -30 to 30
- h_field: float32 [3, 256, 256, 128], P(None, 'gx', 'gy'), may hold values from -30 to 30
- material: int32 [256, 256, 64], P('gx', 'gy'), may hold values from 0 to 3
- permittivity: float32 [4], replicated, may hold values from 1 to 12
- frequencies: float32 [4], replicated, may hold values from 0.6 to 2.4
Outputs:
- e_out: float32 [3, 256, 256, 128], P(None, 'gx', 'gy')
- h_out: float32 [3, 256, 256, 128], P(None, 'gx', 'gy')
- gram: float32 [8, 8], replicated
The draws below stay inside these ranges and needn't reach their ends.
All inputs are finite; a program needn't handle non-finite values.
Results may differ from the reference program's by a relative error of at most 0.000096.
Values sent between devices are 32-bit elements; how exact they have to be, the bound alone decides.
No kernel may reach another device: no remote copies, remote signals or barrier semaphores. Data moves between devices by JAX's collectives and lax.ppermute only.
A program may use at most 64 MiB of HBM per device.

```python
import math
import jax
import jax.numpy as jnp
from jax import lax

NZ = 64
SOURCES = 2
FILTERS = 4
MATERIALS = 4
ITERS = 4
NX = 256
NY = 256


def field_draw(key, salt):
    key = jax.random.fold_in(key, salt)
    first, second = jax.random.split(key)
    xpos = jnp.arange(NX, dtype=jnp.float32) / max(NX - 1, 1)
    ypos = jnp.arange(NY, dtype=jnp.float32) / max(NY - 1, 1)
    root = jnp.sqrt(jnp.float32(3.0))
    envelope = (root ** xpos)[:, None] * (root ** ypos)[None, :]
    common = jnp.clip(jax.random.normal(first, (3, NX, NY, NZ), jnp.float32), -6.0, 6.0)
    own = jnp.clip(jax.random.normal(second, (3, NX, NY, SOURCES * NZ), jnp.float32), -6.0, 6.0)
    mixed = 0.6 * jnp.repeat(common, SOURCES, axis=-1) + 0.8 * own
    return envelope[None, :, :, None] * mixed


def draw_e_field(key, part):
    return field_draw(key, 11)


def draw_h_field(key, part):
    return field_draw(key, 23)


def plant(entries, key, low, largest):
    spot = [jax.random.randint(jax.random.fold_in(key, axis), (), 0, length) for axis, length in enumerate(entries.shape)]
    main_axis = entries.shape.index(max(entries.shape))
    next_to = spot[:main_axis] + [(spot[main_axis] + 1) % entries.shape[main_axis]] + spot[main_axis + 1:]
    return entries.at[tuple(spot)].set(low).at[tuple(next_to)].set(largest)


def setup_inputs(seed: int = 0) -> dict:
    key_of = jax.random.split(jax.random.key(seed), 6)
    e_field = draw_e_field(jax.random.fold_in(key_of[5], 71), 0)
    h_field = draw_h_field(jax.random.fold_in(key_of[5], 71), 0)
    material = plant(jax.random.randint(key_of[2], (NX, NY, NZ), 0, MATERIALS), jax.random.fold_in(key_of[2], 1), 0, MATERIALS - 1).astype(jnp.int32)
    permittivity = jnp.clip(jnp.exp(jax.random.uniform(key_of[3], (MATERIALS,), jnp.float32, math.log(1.0), math.log(12.0))), 1.0, 12.0)
    frequencies = jnp.clip(jax.random.uniform(key_of[4], (FILTERS,), jnp.float32, 0.6, 2.4), 0.6, 2.4)
    return {"e_field": e_field, "h_field": h_field, "material": material, "permittivity": permittivity, "frequencies": frequencies}


TIME_STEP = 0.5


def forward_z(field):
    pad = jnp.zeros(field.shape[:-1] + (SOURCES,), field.dtype)
    return jnp.concatenate([field[..., SOURCES:], pad], axis=-1) - field


def backward_z(field):
    pad = jnp.zeros(field.shape[:-1] + (SOURCES,), field.dtype)
    return field - jnp.concatenate([pad, field[..., :-SOURCES]], axis=-1)


def reference(e_field, h_field, material, permittivity, frequencies):
    onehot = (material[..., None] == jnp.arange(MATERIALS, dtype=jnp.int32)).astype(jnp.float32)
    permit_cell = jnp.sum(onehot * permittivity, axis=-1)
    permit = jnp.repeat(permit_cell, SOURCES, axis=-1)
    scaled = TIME_STEP / permit
    e_x, e_y, e_z = e_field[0], e_field[1], e_field[2]
    h_x, h_y, h_z = h_field[0], h_field[1], h_field[2]
    filtered = jnp.zeros((FILTERS,) + e_field.shape, jnp.float32)
    for step in range(ITERS):
        curl_x = (jnp.roll(e_z, -1, 1) - e_z) - forward_z(e_y)
        curl_y = forward_z(e_x) - (jnp.roll(e_z, -1, 0) - e_z)
        curl_z = (jnp.roll(e_y, -1, 0) - e_y) - (jnp.roll(e_x, -1, 1) - e_x)
        h_x = h_x - TIME_STEP * curl_x
        h_y = h_y - TIME_STEP * curl_y
        h_z = h_z - TIME_STEP * curl_z
        curl_x = (h_z - jnp.roll(h_z, 1, 1)) - backward_z(h_y)
        curl_y = backward_z(h_x) - (h_z - jnp.roll(h_z, 1, 0))
        curl_z = (h_y - jnp.roll(h_y, 1, 0)) - (h_x - jnp.roll(h_x, 1, 1))
        e_x = e_x + scaled * curl_x
        e_y = e_y + scaled * curl_y
        e_z = e_z + scaled * curl_z
        weights = jnp.cos(frequencies * ((step + 1) * TIME_STEP))
        filtered = filtered + weights[:, None, None, None, None] * jnp.stack([e_x, e_y, e_z])[None]
    shaped = filtered.reshape(FILTERS, 3, NX, NY, NZ, SOURCES)
    weighted = shaped * permit_cell[None, None, :, :, :, None]
    pairs = jnp.einsum("kcxyzs,lcxyzt->kslt", weighted, shaped, precision=lax.Precision.HIGHEST)
    gram = pairs.reshape(FILTERS * SOURCES, FILTERS * SOURCES) / (NX * NY * NZ)
    return jnp.stack([e_x, e_y, e_z]), jnp.stack([h_x, h_y, h_z]), gram
```

```python
import jax
import jax.numpy as jnp
from jax import lax
from jax.experimental import pallas as pl
from jax.experimental.pallas import tpu as pltpu
from jax.sharding import PartitionSpec as P

NZ = 64
SOURCES = 2
FILTERS = 4
MATERIALS = 4
ITERS = 4
TIME_STEP = 0.5

BX, BY, LANES = 8, 16, NZ * SOURCES
HALO = ITERS
PX = BX + 2 * HALO
PY = BY + 2 * HALO
XTILES = 49
YTILES = 7 * PX // 2

VMEM = pl.BlockSpec(memory_space=pltpu.VMEM)
SMEM = pl.BlockSpec(memory_space=pltpu.SMEM)
PARAMS = pltpu.CompilerParams(vmem_limit_bytes=32 * 1024 * 1024)


def iota(shape, dim):
    return lax.broadcasted_iota(jnp.int32, shape, dim)


def call(kernel, outs, name, n_in, scratch=(), smem=(), flops=0, size=0):
    return pl.pallas_call(
        kernel,
        out_shape=outs,
        in_specs=[SMEM if i in smem else VMEM for i in range(n_in)],
        out_specs=jax.tree.map(lambda _: VMEM, outs),
        scratch_shapes=list(scratch),
        compiler_params=PARAMS,
        cost_estimate=pl.CostEstimate(flops=flops, bytes_accessed=size, transcendentals=0),
        name=name,
    )


def f32(*shape):
    return jax.ShapeDtypeStruct(shape, jnp.float32)


def pack_x(e_ref, h_ref, m_ref, a_ref, b_ref):
    even = lax.rem(lax.axis_index("gx"), 2) == 0
    row, col = iota((NZ, LANES), 0), iota((NZ, LANES), 1)
    low = (col == row).astype(jnp.bfloat16)
    high = (col == row + NZ).astype(jnp.bfloat16)
    for out, upper in ((a_ref, even), (b_ref, jnp.logical_not(even))):
        wide = jnp.where(upper, BX - HALO, 0)
        narrow = jnp.where(upper, BX - HALO + 1, 0)
        tile = 0
        for ref, c, n, start in (
            (e_ref, 0, 4, wide), (e_ref, 1, 4, wide), (e_ref, 2, 4, wide),
            (h_ref, 0, 3, narrow), (h_ref, 1, 4, wide), (h_ref, 2, 4, wide),
        ):
            out[pl.ds(tile, 2 * n)] = ref[c, pl.ds(start, n)].reshape(2 * n, 8, LANES)
            tile += 2 * n
        for i in range(3):
            cells = m_ref[narrow + i].astype(jnp.float32).astype(jnp.bfloat16)
            out[tile + i] = jnp.dot(cells[:8], low, preferred_element_type=jnp.float32) + jnp.dot(
                cells[8:], high, preferred_element_type=jnp.float32
            )


def look_up(index, table_ref):
    value = jnp.full(index.shape, table_ref[0], jnp.float32)
    for m in range(1, MATERIALS):
        value = jnp.where(index == float(m), table_ref[m], value)
    return value


def own_cells(m_ref, p_ref, permit_ref, scaled_ref):
    row, col = iota((NZ, LANES), 0), iota((NZ, LANES), 1)
    spread = (col // SOURCES == row).astype(jnp.bfloat16)
    cells = m_ref[...].reshape(BX * BY, NZ).astype(jnp.float32).astype(jnp.bfloat16)
    index = jnp.dot(cells, spread, preferred_element_type=jnp.float32)
    permit = look_up(index, p_ref)
    permit_ref[...] = permit.reshape(BX, BY, LANES)
    scaled_ref[...] = (TIME_STEP / permit).reshape(BX, BY, LANES)


def extend_x(e_ref, h_ref, s_ref, a_ref, b_ref, p_ref, ye_ref, yh_ref, ys_ref, ya_ref, yb_ref):
    even = lax.rem(lax.axis_index("gx"), 2) == 0
    row, col = iota((LANES, LANES), 0), iota((LANES, LANES), 1)
    low = (col // SOURCES == row).astype(jnp.bfloat16)
    high = (col // SOURCES == row - NZ).astype(jnp.bfloat16)
    ye_ref[:, :BX] = e_ref[...]
    yh_ref[:, :BX] = h_ref[...]
    ys_ref[:BX] = s_ref[...]
    for src, after in ((a_ref, even), (b_ref, jnp.logical_not(even))):
        wide = jnp.where(after, BX, BX + HALO)
        narrow = jnp.where(after, BX, BX + HALO + 1)
        tile = 0
        for ref, c, n, start in (
            (ye_ref, 0, 4, wide), (ye_ref, 1, 4, wide), (ye_ref, 2, 4, wide),
            (yh_ref, 0, 3, narrow), (yh_ref, 1, 4, wide), (yh_ref, 2, 4, wide),
        ):
            ref[c, pl.ds(start, n)] = src[pl.ds(tile, 2 * n)].reshape(n, BY, LANES)
            tile += 2 * n
        cells = src[pl.ds(tile, 3)].reshape(24, LANES).astype(jnp.bfloat16)
        for half, spread in ((0, low), (8, high)):
            index = jnp.dot(cells, spread, preferred_element_type=jnp.float32)
            value = TIME_STEP / look_up(index, p_ref)
            for i in range(3):
                ys_ref[narrow + i, pl.ds(half, 8)] = value[8 * i : 8 * i + 8]
    zero = jnp.zeros((BY, LANES), jnp.float32)
    yh_ref[0, BX + HALO] = zero
    yh_ref[0, BX + HALO - 1] = zero
    ys_ref[BX + HALO] = zero
    ys_ref[BX + HALO - 1] = zero
    fill_y(ye_ref, yh_ref, ys_ref, ya_ref, yb_ref)


def fill_y(ye_ref, yh_ref, ys_ref, ya_ref, yb_ref):
    even = lax.rem(lax.axis_index("gy"), 2) == 0
    first = iota((8, LANES), 0) < HALO
    for f in range(7):
        ref = (ye_ref, ye_ref, ye_ref, yh_ref, yh_ref, yh_ref)[f].at[f % 3] if f < 6 else ys_ref
        for p in range(PX // 2):
            top = jnp.where(first, pltpu.roll(ref[p, 8:16], HALO, 0), ref[p + PX // 2, 8:16])
            bottom = jnp.where(first, ref[p, 0:8], pltpu.roll(ref[p + PX // 2, 0:8], HALO, 0))
            ya_ref[f * 8 + p] = jnp.where(even, top, bottom)
            yb_ref[f * 8 + p] = jnp.where(even, bottom, top)


def steps(xe_ref, xh_ref, xs_ref, permit_ref, ya_ref, yb_ref, w_ref, e_ref, h_ref, part_ref, ee, hh, ss):
    even = lax.rem(lax.axis_index("gy"), 2) == 0
    first = iota((8, LANES), 0) < HALO
    for f in range(7):
        src = xe_ref.at[f % 3] if f < 3 else xh_ref.at[f % 3] if f < 6 else xs_ref
        dst = ee.at[0, f % 3] if f < 3 else hh.at[f % 3] if f < 6 else ss
        dst[:, :BY] = src[...]
        for p in range(PX // 2):
            a, b = ya_ref[f * 8 + p], yb_ref[f * 8 + p]
            after, before = jnp.where(even, a, b), jnp.where(even, b, a)
            dst[p, BY:PY] = jnp.where(first, after, pltpu.roll(before, HALO, 0))
            dst[p + PX // 2, BY:PY] = jnp.where(first, pltpu.roll(after, HALO, 0), before)

    lane = iota((PY, LANES), 1)
    not_last, not_first = lane < LANES - SOURCES, lane >= SOURCES

    def up_z(v):
        return jnp.where(not_last, pltpu.roll(v, LANES - SOURCES, 1), 0.0)

    def down_z(v):
        return jnp.where(not_first, pltpu.roll(v, SOURCES, 1), 0.0)

    def new_h(n, i):
        p, q = i & (PX - 1), (i + 1) & (PX - 1)
        e_x, e_y, e_z = ee[n, 0, p], ee[n, 1, p], ee[n, 2, p]
        e_yn, e_zn = ee[n, 1, q], ee[n, 2, q]
        h_x = hh[0, p] - TIME_STEP * ((pltpu.roll(e_z, PY - 1, 0) - e_z) - (up_z(e_y) - e_y))
        h_y = hh[1, p] - TIME_STEP * ((up_z(e_x) - e_x) - (e_zn - e_z))
        h_z = hh[2, p] - TIME_STEP * ((e_yn - e_y) - (pltpu.roll(e_x, PY - 1, 0) - e_x))
        hh[0, p], hh[1, p], hh[2, p] = h_x, h_y, h_z
        return h_x, h_y, h_z

    def new_e(n, i, h, h_before):
        p = i & (PX - 1)
        h_x, h_y, h_z = h
        h_yb, h_zb = h_before
        s = ss[p]
        e_x = ee[n, 0, p] + s * ((h_z - pltpu.roll(h_z, 1, 0)) - (h_y - down_z(h_y)))
        e_y = ee[n, 1, p] + s * ((h_x - down_z(h_x)) - (h_z - h_zb))
        e_z = ee[n, 2, p] + s * ((h_y - h_yb) - (h_x - pltpu.roll(h_x, 1, 0)))
        ee[n + 1, 0, p], ee[n + 1, 1, p], ee[n + 1, 2, p] = e_x, e_y, e_z

    for n in range(ITERS):
        left, right = -(HALO - n), BX + HALO - 1 - n
        h = new_h(n, jnp.int32(left))

        def plane(i, before, n=n):
            h = new_h(n, i)
            new_e(n, i, h, before)
            return h[1], h[2]

        lax.fori_loop(left + 1, right, plane, (h[1], h[2]))

    e_ref[...] = ee[ITERS, :, :BX, :BY]
    h_ref[...] = hh[:, :BX, :BY]

    even_lane = iota((BY, LANES), 1) % 2 == 0

    def gram(j, sums):
        c, p = j // BX, j % BX
        e = [ee[n + 1, c, p, pl.ds(0, BY)] for n in range(ITERS)]
        permit = permit_ref[p]
        f = [sum(w_ref[n, k] * e[n] for n in range(ITERS)) for k in range(FILTERS)]
        g = [v * permit for v in f]
        o = [jnp.where(even_lane, pltpu.roll(v, LANES - 1, 1), pltpu.roll(v, 1, 1)) for v in g]
        new = []
        for right in (g, o):
            for k in range(FILTERS):
                for l in range(k, FILTERS):
                    v = f[k] * right[l]
                    new.append(v[:8] + v[8:])
        return tuple(s + v for s, v in zip(sums, new))

    zero = jnp.zeros((8, LANES), jnp.float32)
    sums = lax.fori_loop(0, 3 * BX, gram, (zero,) * 20)
    row_of = iota((32, LANES), 0)
    rows = jnp.zeros((32, LANES), jnp.float32)
    at = 0
    for cross in range(2):
        for k in range(FILTERS):
            for l in range(k, FILTERS):
                line = jnp.sum(sums[at], axis=0, keepdims=True)
                rows = jnp.where(row_of == cross * 16 + k * 4 + l, line, rows)
                at += 1

    def entry(shape):
        j = iota(shape, 1)
        k, s, l, t = (j >> 4) & 3, (j >> 3) & 1, (j >> 1) & 3, j & 1
        source = jnp.where(k <= l, s, t)
        which = jnp.where(s == t, 0, 16) + jnp.minimum(k, l) * 4 + jnp.maximum(k, l)
        return jnp.where(j < 64, which, -1), source

    lane_source = (iota((LANES, LANES), 0) & 1 == entry((LANES, LANES))[1]).astype(jnp.float32)
    totals = jnp.dot(rows, lane_source, precision=lax.Precision.HIGHEST, preferred_element_type=jnp.float32)
    vector = jnp.sum(jnp.where(row_of == entry((32, LANES))[0], totals, 0.0), axis=0, keepdims=True)
    part_ref[...] = jnp.broadcast_to(vector[None], part_ref.shape)


def add_up(in_ref, out_ref):
    out_ref[...] = jnp.broadcast_to(jnp.sum(in_ref[...], axis=0, keepdims=True), out_ref.shape)


def finish(cells, in_ref, out_ref):
    vector = jnp.broadcast_to(jnp.sum(in_ref[...], axis=0), (8, LANES))
    picked = jnp.where(iota((8, LANES), 1) // 8 == iota((8, LANES), 0), vector, 0.0)
    fold = (iota((LANES, LANES), 0) % 8 == iota((LANES, LANES), 1)).astype(jnp.float32)
    total = jnp.dot(picked, fold, precision=lax.Precision.HIGHEST, preferred_element_type=jnp.float32)
    out_ref[...] = total[:, :8] / cells


def swap_pairs(count, odd):
    if not odd:
        return [(i, i ^ 1) for i in range(count)]
    return [(i, (i + 1) % count if i % 2 else (i - 1) % count) for i in range(count)]


def sum_groups(n_gx, n_gy):
    planes, columns = {}, {}
    for gx in range(n_gx):
        for gy in range(n_gy):
            y, z_high, x = gx // 8, (gx // 4) % 2, gx % 4
            z, core = z_high * 8 + gy // 2, gy % 2
            planes.setdefault(z, []).append(gx * n_gy + gy)
            columns.setdefault((x, y, core), []).append(gx * n_gy + gy)
    return list(planes.values()), list(columns.values())


def body(e_field, h_field, material, permittivity, frequencies):
    n_gx, n_gy = lax.axis_size("gx"), lax.axis_size("gy")
    weights = jnp.cos(frequencies[None, :] * (jnp.arange(1, ITERS + 1, dtype=jnp.float32)[:, None] * TIME_STEP))
    send_a, send_b = call(pack_x, (f32(XTILES, 8, LANES),) * 2, "pack_x", 3, size=1 << 20)(e_field, h_field, material)
    got_a = lax.ppermute(send_a, "gx", swap_pairs(n_gx, False))
    got_b = lax.ppermute(send_b, "gx", swap_pairs(n_gx, True))
    permit, scaled = call(own_cells, (f32(BX, BY, LANES),) * 2, "own_cells", 2, smem=(1,), size=1 << 18)(
        material, permittivity
    )
    ext = (f32(3, PX, BY, LANES), f32(3, PX, BY, LANES), f32(PX, BY, LANES), f32(YTILES, 8, LANES), f32(YTILES, 8, LANES))
    ext_e, ext_h, ext_s, send_a, send_b = call(extend_x, ext, "extend_x", 6, smem=(5,), size=1 << 21)(
        e_field, h_field, scaled, got_a, got_b, permittivity
    )
    got_a = lax.ppermute(send_a, "gy", swap_pairs(n_gy, False))
    got_b = lax.ppermute(send_b, "gy", swap_pairs(n_gy, True))
    planes, columns = sum_groups(n_gx, n_gy)
    n_plane, n_column = len(planes[0]), len(columns[0])
    scratch = (
        pltpu.VMEM((ITERS + 1, 3, PX, PY, LANES), jnp.float32),
        pltpu.VMEM((3, PX, PY, LANES), jnp.float32),
        pltpu.VMEM((PX, PY, LANES), jnp.float32),
    )
    outs = (f32(3, BX, BY, LANES), f32(3, BX, BY, LANES), f32(n_plane, 1, LANES))
    e_out, h_out, part = call(steps, outs, "steps", 7, scratch=scratch, smem=(6,), flops=1 << 24, size=1 << 22)(
        ext_e, ext_h, ext_s, permit, got_a, got_b, weights
    )
    both = ("gx", "gy")
    part = lax.all_to_all(part, both, 0, 0, axis_index_groups=planes, tiled=True)
    part = call(add_up, f32(n_column, 1, LANES), "add_up", 1, size=1 << 14)(part)
    part = lax.all_to_all(part, both, 0, 0, axis_index_groups=columns, tiled=True)
    cells = float(BX * n_gx * BY * n_gy * NZ)

    def last(in_ref, out_ref):
        finish(cells, in_ref, out_ref)

    gram = call(last, f32(8, 8), "finish", 1, size=1 << 14)(part)
    return e_out, h_out, gram


def solution(mesh):
    in_specs = (P(None, "gx", "gy", None), P(None, "gx", "gy", None), P("gx", "gy", None), P(), P())
    out_specs = (P(None, "gx", "gy", None), P(None, "gx", "gy", None), P())
    return jax.shard_map(body, mesh=mesh, in_specs=in_specs, out_specs=out_specs, check_vma=False)
```

```python
import jax
import jax.numpy as jnp
from jax import lax
from jax.experimental import pallas as pl
from jax.experimental.pallas import tpu as pltpu
from jax.sharding import PartitionSpec as P

NZ = 64
SOURCES = 2
FILTERS = 4
MATERIALS = 4
ITERS = 4
TIME_STEP = 0.5

BX, BY, LANES = 8, 16, NZ * SOURCES
HALO = ITERS
PX = BX + 2 * HALO
PY = BY + 2 * HALO
XTILES = 49
YTILES = 7 * BX // 2

VMEM = pl.BlockSpec(memory_space=pltpu.VMEM)
HBM = pl.BlockSpec(memory_space=pltpu.HBM)
SMEM = pl.BlockSpec(memory_space=pltpu.SMEM)
PARAMS = pltpu.CompilerParams(vmem_limit_bytes=32 * 1024 * 1024)


def iota(shape, dim):
    return lax.broadcasted_iota(jnp.int32, shape, dim)


def call(kernel, outs, name, n_in, scratch=(), smem=(), hbm=(), hbm_out=(), flops=0, size=0):
    out_specs = tuple(HBM if i in hbm_out else VMEM for i in range(len(outs))) if isinstance(outs, tuple) else VMEM
    return pl.pallas_call(
        kernel,
        out_shape=outs,
        in_specs=[SMEM if i in smem else HBM if i in hbm else VMEM for i in range(n_in)],
        out_specs=out_specs,
        scratch_shapes=list(scratch),
        compiler_params=PARAMS,
        cost_estimate=pl.CostEstimate(flops=flops, bytes_accessed=size, transcendentals=0),
        name=name,
    )


def f32(*shape):
    return jax.ShapeDtypeStruct(shape, jnp.float32)


def x_parts(e, h, wide, narrow):
    return ((e, 0, 4, wide), (e, 1, 4, wide), (e, 2, 4, wide), (h, 0, 3, narrow), (h, 1, 4, wide), (h, 2, 4, wide))


def pack_x(e_ref, h_ref, m_ref, a_ref, b_ref, edge, sems):
    even = lax.rem(lax.axis_index("gx"), 2) == 0
    copies = []
    for side, (out, upper) in enumerate(((a_ref, even), (b_ref, jnp.logical_not(even)))):
        wide = jnp.where(upper, BX - HALO, 0)
        narrow = jnp.where(upper, BX - HALO + 1, 0)
        copies.append(pltpu.make_async_copy(m_ref.at[pl.ds(narrow, 3)], edge.at[side], sems.at[side, 6]))
        row = 0
        for i, (ref, c, n, start) in enumerate(x_parts(e_ref, h_ref, wide, narrow)):
            src = ref.at[c, pl.ds(pl.multiple_of(start * BY, BY), n * BY)]
            copies.append(pltpu.make_async_copy(src, out.at[pl.ds(row, n * BY)], sems.at[side, i]))
            row += n * BY
    for copy in copies:
        copy.start()
    r, col = iota((NZ, LANES), 0), iota((NZ, LANES), 1)
    low = (col == r).astype(jnp.bfloat16)
    high = (col == r + NZ).astype(jnp.bfloat16)
    for side, out in enumerate((a_ref, b_ref)):
        copies[7 * side].wait()
        for i in range(3):
            cells = edge[side, i].astype(jnp.float32).astype(jnp.bfloat16)
            out[pl.ds(8 * (XTILES - 3 + i), 8)] = jnp.dot(
                cells[:8], low, preferred_element_type=jnp.float32
            ) + jnp.dot(cells[8:], high, preferred_element_type=jnp.float32)
    for i, copy in enumerate(copies):
        if i % 7:
            copy.wait()


def look_up(index, table_ref):
    value = jnp.full(index.shape, table_ref[0], jnp.float32)
    for m in range(1, MATERIALS):
        value = jnp.where(index == float(m), table_ref[m], value)
    return value


def own_cells(m_ref, p_ref, permit_ref, scaled_ref):
    row, col = iota((NZ, LANES), 0), iota((NZ, LANES), 1)
    spread = (col // SOURCES == row).astype(jnp.bfloat16)
    cells = m_ref[...].reshape(BX * BY, NZ).astype(jnp.float32).astype(jnp.bfloat16)
    index = jnp.dot(cells, spread, preferred_element_type=jnp.float32)
    permit = look_up(index, p_ref)
    permit_ref[...] = permit.reshape(BX, BY, LANES)
    scaled_ref[...] = (TIME_STEP / permit).reshape(BX, BY, LANES)


def pack_y(refs, ya_ref, yb_ref):
    even = lax.rem(lax.axis_index("gy"), 2) == 0
    first = iota((8, LANES), 0) < HALO
    for f, ref in enumerate(refs):
        for p in range(4):
            top = jnp.where(first, pltpu.roll(ref[p, 8:16], HALO, 0), ref[p + 4, 8:16])
            bottom = jnp.where(first, ref[p, 0:8], pltpu.roll(ref[p + 4, 0:8], HALO, 0))
            ya_ref[f * 4 + p] = jnp.where(even, top, bottom)
            yb_ref[f * 4 + p] = jnp.where(even, bottom, top)


def unpack_y(refs, base, ya_ref, yb_ref):
    even = lax.rem(lax.axis_index("gy"), 2) == 0
    first = iota((8, LANES), 0) < HALO
    for f, ref in enumerate(refs):
        for p in range(4):
            a, b = ya_ref[f * 4 + p], yb_ref[f * 4 + p]
            after, before = jnp.where(even, a, b), jnp.where(even, b, a)
            ref[base + p, BY:PY] = jnp.where(first, after, pltpu.roll(before, HALO, 0))
            ref[base + p + 4, BY:PY] = jnp.where(first, pltpu.roll(after, HALO, 0), before)


def fields(e, h, s):
    return [e.at[c] for c in range(3)] + [h.at[c] for c in range(3)] + [s]


def own_rows(e_ref, h_ref, s_ref, ya_ref, yb_ref):
    pack_y(fields(e_ref, h_ref, s_ref), ya_ref, yb_ref)


def ghost_planes(a_ref, b_ref, p_ref, e_ref, h_ref, s_ref, ya_ref, yb_ref):
    even = lax.rem(lax.axis_index("gx"), 2) == 0
    r, col = iota((LANES, LANES), 0), iota((LANES, LANES), 1)
    low = (col // SOURCES == r).astype(jnp.bfloat16)
    high = (col // SOURCES == r - NZ).astype(jnp.bfloat16)
    for src, after in ((a_ref, even), (b_ref, jnp.logical_not(even))):
        wide = jnp.where(after, 0, HALO)
        narrow = jnp.where(after, 0, HALO + 1)
        row = 0
        for ref, c, n, start in x_parts(e_ref, h_ref, wide, narrow):
            ref[c, pl.ds(start, n)] = src[pl.ds(row, n * BY)].reshape(n, BY, LANES)
            row += n * BY
        cells = src[pl.ds(row, 24)].astype(jnp.bfloat16)
        for half, spread in ((0, low), (8, high)):
            index = jnp.dot(cells, spread, preferred_element_type=jnp.float32)
            value = TIME_STEP / look_up(index, p_ref)
            for i in range(3):
                s_ref[narrow + i, pl.ds(half, 8)] = value[8 * i : 8 * i + 8]
    zero = jnp.zeros((BY, LANES), jnp.float32)
    for ref in (h_ref.at[0], s_ref):
        ref[HALO - 1] = zero
        ref[HALO] = zero
    pack_y(fields(e_ref, h_ref, s_ref), ya_ref, yb_ref)


def steps(
    own_e, own_h, own_s, permit_ref, ghost_e, ghost_h, ghost_s, ya1, yb1, ya2, yb2, w_ref,
    e_out, h_out, part_ref, ee, hh, ss, sems,
):
    extended = fields(ee.at[0], hh, ss)
    for dst, own, ghost in zip(extended, fields(own_e, own_h, own_s), fields(ghost_e, ghost_h, ghost_s)):
        dst[:BX, :BY] = own[...]
        dst[BX:, :BY] = ghost[...]
    unpack_y(extended, 0, ya1, yb1)
    unpack_y(extended, BX, ya2, yb2)

    lane = iota((PY, LANES), 1)
    not_last, not_first = lane < LANES - SOURCES, lane >= SOURCES

    def up_z(v):
        return jnp.where(not_last, pltpu.roll(v, LANES - SOURCES, 1), 0.0)

    def down_z(v):
        return jnp.where(not_first, pltpu.roll(v, SOURCES, 1), 0.0)

    def new_h(n, i):
        p, q = i & (PX - 1), (i + 1) & (PX - 1)
        e_x, e_y, e_z = ee[n, 0, p], ee[n, 1, p], ee[n, 2, p]
        e_yn, e_zn = ee[n, 1, q], ee[n, 2, q]
        h_x = hh[0, p] - TIME_STEP * ((pltpu.roll(e_z, PY - 1, 0) - e_z) - (up_z(e_y) - e_y))
        h_y = hh[1, p] - TIME_STEP * ((up_z(e_x) - e_x) - (e_zn - e_z))
        h_z = hh[2, p] - TIME_STEP * ((e_yn - e_y) - (pltpu.roll(e_x, PY - 1, 0) - e_x))
        hh[0, p], hh[1, p], hh[2, p] = h_x, h_y, h_z
        return h_x, h_y, h_z

    def new_e(n, i, h, h_before):
        p = i & (PX - 1)
        h_x, h_y, h_z = h
        h_yb, h_zb = h_before
        s = ss[p]
        e_x = ee[n, 0, p] + s * ((h_z - pltpu.roll(h_z, 1, 0)) - (h_y - down_z(h_y)))
        e_y = ee[n, 1, p] + s * ((h_x - down_z(h_x)) - (h_z - h_zb))
        e_z = ee[n, 2, p] + s * ((h_y - h_yb) - (h_x - pltpu.roll(h_x, 1, 0)))
        ee[n + 1, 0, p], ee[n + 1, 1, p], ee[n + 1, 2, p] = e_x, e_y, e_z

    for n in range(ITERS):
        left, right = -(HALO - n), BX + HALO - 1 - n
        h = new_h(n, jnp.int32(left))

        def plane(i, before, n=n):
            h = new_h(n, i)
            new_e(n, i, h, before)
            return h[1], h[2]

        lax.fori_loop(left + 1, right, plane, (h[1], h[2]), unroll=True)

    own = (slice(None), pl.ds(0, BX), pl.ds(0, BY))
    copies = [
        pltpu.make_async_copy(ee.at[(ITERS,) + own], e_out, sems.at[0]),
        pltpu.make_async_copy(hh.at[own], h_out, sems.at[1]),
    ]
    for copy in copies:
        copy.start()

    even_lane = iota((BY, LANES), 1) % 2 == 0

    def gram(j, sums):
        c, p = j // BX, j % BX
        e = [ee[n + 1, c, p, pl.ds(0, BY)] for n in range(ITERS)]
        permit = permit_ref[p]
        f = [sum(w_ref[n, k] * e[n] for n in range(ITERS)) for k in range(FILTERS)]
        g = [v * permit for v in f]
        o = [jnp.where(even_lane, pltpu.roll(v, LANES - 1, 1), pltpu.roll(v, 1, 1)) for v in g]
        new = []
        for right in (g, o):
            for k in range(FILTERS):
                for l in range(k, FILTERS):
                    v = f[k] * right[l]
                    new.append(v[:8] + v[8:])
        return tuple(s + v for s, v in zip(sums, new))

    zero = jnp.zeros((8, LANES), jnp.float32)
    sums = lax.fori_loop(0, 3 * BX, gram, (zero,) * 20, unroll=4)
    row_of = iota((32, LANES), 0)
    rows = jnp.zeros((32, LANES), jnp.float32)
    at = 0
    for cross in range(2):
        for k in range(FILTERS):
            for l in range(k, FILTERS):
                line = jnp.sum(sums[at], axis=0, keepdims=True)
                rows = jnp.where(row_of == cross * 16 + k * 4 + l, line, rows)
                at += 1

    def entry(shape):
        j = iota(shape, 1)
        k, s, l, t = (j >> 4) & 3, (j >> 3) & 1, (j >> 1) & 3, j & 1
        source = jnp.where(k <= l, s, t)
        which = jnp.where(s == t, 0, 16) + jnp.minimum(k, l) * 4 + jnp.maximum(k, l)
        return jnp.where(j < 64, which, -1), source

    lane_source = (iota((LANES, LANES), 0) & 1 == entry((LANES, LANES))[1]).astype(jnp.float32)
    totals = jnp.dot(rows, lane_source, precision=lax.Precision.HIGHEST, preferred_element_type=jnp.float32)
    vector = jnp.sum(jnp.where(row_of == entry((32, LANES))[0], totals, 0.0), axis=0, keepdims=True)
    part_ref[...] = jnp.broadcast_to(vector[None], part_ref.shape)
    for copy in copies:
        copy.wait()


def add_up(in_ref, out_ref):
    out_ref[...] = jnp.broadcast_to(jnp.sum(in_ref[...], axis=0, keepdims=True), out_ref.shape)


def finish(cells, in_ref, out_ref):
    vector = jnp.broadcast_to(jnp.sum(in_ref[...], axis=0), (8, LANES))
    picked = jnp.where(iota((8, LANES), 1) // 8 == iota((8, LANES), 0), vector, 0.0)
    fold = (iota((LANES, LANES), 0) % 8 == iota((LANES, LANES), 1)).astype(jnp.float32)
    total = jnp.dot(picked, fold, precision=lax.Precision.HIGHEST, preferred_element_type=jnp.float32)
    out_ref[...] = total[:, :8] / cells


def swap_pairs(count, odd):
    if not odd:
        return [(i, i ^ 1) for i in range(count)]
    return [(i, (i + 1) % count if i % 2 else (i - 1) % count) for i in range(count)]


def sum_groups(n_gx, n_gy):
    planes, columns = {}, {}
    for gx in range(n_gx):
        for gy in range(n_gy):
            y, z_high, x = gx // 8, (gx // 4) % 2, gx % 4
            z, core = z_high * 8 + gy // 2, gy % 2
            planes.setdefault(z, []).append(gx * n_gy + gy)
            columns.setdefault((x, y, core), []).append(gx * n_gy + gy)
    return list(planes.values()), list(columns.values())


def body(e_field, h_field, material, permittivity, frequencies):
    n_gx, n_gy = lax.axis_size("gx"), lax.axis_size("gy")
    weights = jnp.cos(frequencies[None, :] * (jnp.arange(1, ITERS + 1, dtype=jnp.float32)[:, None] * TIME_STEP))
    x_message = (f32(XTILES * 8, LANES),) * 2
    y_message = (f32(YTILES, 8, LANES),) * 2
    scratch = (pltpu.VMEM((2, 3, BY, NZ), jnp.int32), pltpu.SemaphoreType.DMA((2, 7)))
    send_a, send_b = call(pack_x, x_message, "pack_x", 3, scratch=scratch, hbm=(0, 1, 2), size=1 << 20)(
        *(
            pltpu.with_memory_space_constraint(v, pltpu.HBM)
            for v in (e_field.reshape(3, BX * BY, LANES), h_field.reshape(3, BX * BY, LANES), material)
        )
    )
    got_a = lax.ppermute(send_a, "gx", swap_pairs(n_gx, False))
    got_b = lax.ppermute(send_b, "gx", swap_pairs(n_gx, True))
    permit, scaled = call(own_cells, (f32(BX, BY, LANES),) * 2, "own_cells", 2, smem=(1,), size=1 << 18)(
        material, permittivity
    )
    send_a, send_b = call(own_rows, y_message, "own_rows", 3, size=1 << 20)(e_field, h_field, scaled)
    ya1 = lax.ppermute(send_a, "gy", swap_pairs(n_gy, False))
    yb1 = lax.ppermute(send_b, "gy", swap_pairs(n_gy, True))
    ghosts = (f32(3, 2 * HALO, BY, LANES), f32(3, 2 * HALO, BY, LANES), f32(2 * HALO, BY, LANES)) + y_message
    ghost_e, ghost_h, ghost_s, send_a, send_b = call(ghost_planes, ghosts, "ghost_planes", 3, smem=(2,), size=1 << 20)(
        got_a, got_b, permittivity
    )
    ya2 = lax.ppermute(send_a, "gy", swap_pairs(n_gy, False))
    yb2 = lax.ppermute(send_b, "gy", swap_pairs(n_gy, True))
    planes, columns = sum_groups(n_gx, n_gy)
    n_plane, n_column = len(planes[0]), len(columns[0])
    scratch = (
        pltpu.VMEM((ITERS + 1, 3, PX, PY, LANES), jnp.float32),
        pltpu.VMEM((3, PX, PY, LANES), jnp.float32),
        pltpu.VMEM((PX, PY, LANES), jnp.float32),
        pltpu.SemaphoreType.DMA((2,)),
    )
    outs = (f32(3, BX, BY, LANES), f32(3, BX, BY, LANES), f32(n_plane, 1, LANES))
    e_out, h_out, part = call(
        steps, outs, "steps", 12, scratch=scratch, smem=(11,), hbm_out=(0, 1), flops=1 << 24, size=1 << 22
    )(e_field, h_field, scaled, permit, ghost_e, ghost_h, ghost_s, ya1, yb1, ya2, yb2, weights)
    both = ("gx", "gy")
    part = lax.all_to_all(part, both, 0, 0, axis_index_groups=planes, tiled=True)
    part = call(add_up, f32(n_column, 1, LANES), "add_up", 1, size=1 << 14)(part)
    part = lax.all_to_all(part, both, 0, 0, axis_index_groups=columns, tiled=True)
    cells = float(BX * n_gx * BY * n_gy * NZ)

    def last(in_ref, out_ref):
        finish(cells, in_ref, out_ref)

    gram = call(last, f32(8, 8), "finish", 1, size=1 << 14)(part)
    return e_out, h_out, gram


def solution(mesh):
    in_specs = (P(None, "gx", "gy", None), P(None, "gx", "gy", None), P("gx", "gy", None), P(), P())
    out_specs = (P(None, "gx", "gy", None), P(None, "gx", "gy", None), P())
    return jax.shard_map(body, mesh=mesh, in_specs=in_specs, out_specs=out_specs, check_vma=False)
```

```python
import jax
import jax.numpy as jnp
from jax import lax
from jax.experimental import pallas as pl
from jax.experimental.pallas import tpu as pltpu
from jax.sharding import PartitionSpec as P

NZ = 64
SOURCES = 2
FILTERS = 4
MATERIALS = 4
ITERS = 4
TIME_STEP = 0.5

BX, BY, LANES = 8, 16, NZ * SOURCES
HALO = ITERS
PX = BX + 2 * HALO
PY = BY + 2 * HALO
XTILES = 49

VMEM = pl.BlockSpec(memory_space=pltpu.VMEM)
HBM = pl.BlockSpec(memory_space=pltpu.HBM)
SMEM = pl.BlockSpec(memory_space=pltpu.SMEM)
PARAMS = pltpu.CompilerParams(vmem_limit_bytes=32 * 1024 * 1024)


def iota(shape, dim):
    return lax.broadcasted_iota(jnp.int32, shape, dim)


def call(kernel, outs, name, n_in, scratch=(), smem=(), hbm=(), hbm_out=(), flops=0, size=0):
    out_specs = tuple(HBM if i in hbm_out else VMEM for i in range(len(outs))) if isinstance(outs, tuple) else VMEM
    return pl.pallas_call(
        kernel,
        out_shape=outs,
        in_specs=[SMEM if i in smem else HBM if i in hbm else VMEM for i in range(n_in)],
        out_specs=out_specs,
        scratch_shapes=list(scratch),
        compiler_params=PARAMS,
        cost_estimate=pl.CostEstimate(flops=flops, bytes_accessed=size, transcendentals=0),
        name=name,
    )


def f32(*shape):
    return jax.ShapeDtypeStruct(shape, jnp.float32)


def x_parts(e, h, wide, narrow):
    return ((e, 0, 4, wide), (e, 1, 4, wide), (e, 2, 4, wide), (h, 0, 3, narrow), (h, 1, 4, wide), (h, 2, 4, wide))


def pack_x(e_ref, h_ref, m_ref, a_ref, b_ref, edge, sems):
    even = lax.rem(lax.axis_index("gx"), 2) == 0
    copies = []
    for side, (out, upper) in enumerate(((a_ref, even), (b_ref, jnp.logical_not(even)))):
        wide = jnp.where(upper, BX - HALO, 0)
        narrow = jnp.where(upper, BX - HALO + 1, 0)
        copies.append(pltpu.make_async_copy(m_ref.at[pl.ds(narrow, 3)], edge.at[side], sems.at[side, 6]))
        row = 0
        for i, (ref, c, n, start) in enumerate(x_parts(e_ref, h_ref, wide, narrow)):
            src = ref.at[c, pl.ds(pl.multiple_of(start * BY, BY), n * BY)]
            copies.append(pltpu.make_async_copy(src, out.at[pl.ds(row, n * BY)], sems.at[side, i]))
            row += n * BY
    for copy in copies:
        copy.start()
    r, col = iota((NZ, LANES), 0), iota((NZ, LANES), 1)
    low = (col == r).astype(jnp.bfloat16)
    high = (col == r + NZ).astype(jnp.bfloat16)
    for side, out in enumerate((a_ref, b_ref)):
        copies[7 * side].wait()
        for i in range(3):
            cells = edge[side, i].astype(jnp.float32).astype(jnp.bfloat16)
            out[pl.ds(8 * (XTILES - 3 + i), 8)] = jnp.dot(
                cells[:8], low, preferred_element_type=jnp.float32
            ) + jnp.dot(cells[8:], high, preferred_element_type=jnp.float32)
    for i, copy in enumerate(copies):
        if i % 7:
            copy.wait()


def look_up(index, table_ref):
    value = jnp.full(index.shape, table_ref[0], jnp.float32)
    for m in range(1, MATERIALS):
        value = jnp.where(index == float(m), table_ref[m], value)
    return value


def spread(rows, offset):
    shape = (rows, LANES)
    return (iota(shape, 1) // SOURCES + offset == iota(shape, 0)).astype(jnp.bfloat16)


def own_cells(m_ref, p_ref, permit_ref, scaled_ref):
    cells = m_ref[...].reshape(BX * BY, NZ).astype(jnp.float32).astype(jnp.bfloat16)
    permit = look_up(jnp.dot(cells, spread(NZ, 0), preferred_element_type=jnp.float32), p_ref)
    permit_ref[...] = permit.reshape(BX, BY, LANES)
    scaled_ref[...] = (TIME_STEP / permit).reshape(BX, BY, LANES)


def fill_ghosts(src, after, p_ref, e_ref, h_ref, s_ref):
    narrow = jnp.where(after, 0, 1)
    row = 0
    for ref, c, n, start in x_parts(e_ref, h_ref, 0, narrow):
        ref[c, pl.ds(start, n)] = src[pl.ds(row, n * BY)].reshape(n, BY, LANES)
        row += n * BY
    cells = src[pl.ds(row, 24)].astype(jnp.bfloat16)
    for half in range(2):
        index = jnp.dot(cells, spread(LANES, half * NZ), preferred_element_type=jnp.float32)
        value = TIME_STEP / look_up(index, p_ref)
        for i in range(3):
            s_ref[narrow + i, pl.ds(8 * half, 8)] = value[8 * i : 8 * i + 8]
    unused = jnp.where(after, 3, 0)
    h_ref[0, unused] = jnp.zeros((BY, LANES), jnp.float32)
    s_ref[unused] = jnp.zeros((BY, LANES), jnp.float32)


def edge_rows(ref, low, high):
    first = iota((8, LANES), 0) < HALO
    top = jnp.where(first, pltpu.roll(ref[low, 8:16], HALO, 0), ref[high, 8:16])
    bottom = jnp.where(first, ref[low, 0:8], pltpu.roll(ref[high, 0:8], HALO, 0))
    return top, bottom


def pack_y(parts, ya_ref, yb_ref):
    even = lax.rem(lax.axis_index("gy"), 2) == 0
    for tile, (ref, low, high) in enumerate(parts):
        top, bottom = edge_rows(ref, low, high)
        ya_ref[tile] = jnp.where(even, top, bottom)
        yb_ref[tile] = jnp.where(even, bottom, top)


def unpack_y(parts, ya_ref, yb_ref, other=None):
    even = lax.rem(lax.axis_index("gy"), 2) == 0
    wraps = lax.rem(lax.axis_index("gy") + 1, lax.axis_size("gy")) < 2
    first = iota((8, LANES), 0) < HALO
    for tile, (ref, low, high) in enumerate(parts):
        a, b = ya_ref[tile], yb_ref[tile]
        if other is not None:
            b = jnp.where(wraps, other[tile], b)
        after, before = jnp.where(even, a, b), jnp.where(even, b, a)
        ref[low, BY:PY] = jnp.where(first, after, pltpu.roll(before, HALO, 0))
        ref[high, BY:PY] = jnp.where(first, pltpu.roll(after, HALO, 0), before)


def fields(e, h, s):
    return [e.at[c] for c in range(3)] + [h.at[c] for c in range(3)] + [s]


def pairs_of(refs, planes, base=0):
    return [(ref, base + p, base + p + planes // 2) for ref in refs for p in range(planes // 2)]


def near_side(e_ref, h_ref, s_ref, a_ref, p_ref, ge_ref, gh_ref, gs_ref, ya_ref, yb_ref, corner_ref):
    even = lax.rem(lax.axis_index("gx"), 2) == 0
    fill_ghosts(a_ref, even, p_ref, ge_ref, gh_ref, gs_ref)
    own = fields(e_ref, h_ref, s_ref)
    pack_y(pairs_of(own, BX) + pairs_of(fields(ge_ref, gh_ref, gs_ref), HALO), ya_ref, yb_ref)
    start = jnp.where(even, 0, BX - HALO)
    upper = lax.rem(lax.axis_index("gy"), 2) == 1
    for tile, (ref, low, high) in enumerate(pairs_of(own, HALO, start)):
        top, bottom = edge_rows(ref, low, high)
        corner_ref[tile] = jnp.where(upper, top, bottom)


def far_side(b_ref, p_ref, ge_ref, gh_ref, gs_ref, ya_ref, yb_ref):
    odd = lax.rem(lax.axis_index("gx"), 2) == 1
    fill_ghosts(b_ref, odd, p_ref, ge_ref, gh_ref, gs_ref)
    pack_y(pairs_of(fields(ge_ref, gh_ref, gs_ref), HALO), ya_ref, yb_ref)


def steps(
    own_e, own_h, own_s, permit_ref, ae, ah, sa, be, bh, sb, ya1, yb1, ya2, yb2, corner, w_ref,
    e_out, h_out, part_ref, ee, hh, ss, sems,
):
    even = lax.rem(lax.axis_index("gx"), 2) == 0
    base_a, base_b = jnp.where(even, BX, BX + HALO), jnp.where(even, BX + HALO, BX)
    extended = fields(ee.at[0], hh, ss)
    for dst, own, a, b in zip(extended, fields(own_e, own_h, own_s), fields(ae, ah, sa), fields(be, bh, sb)):
        dst[:BX, :BY] = own[...]
        dst[pl.ds(base_a, HALO), :BY] = a[...]
        dst[pl.ds(base_b, HALO), :BY] = b[...]
    unpack_y(pairs_of(extended, BX) + pairs_of(extended, HALO, base_a), ya1, yb1)
    unpack_y(pairs_of(extended, HALO, base_b), ya2, yb2, corner)

    lane = iota((PY, LANES), 1)
    not_last, not_first = lane < LANES - SOURCES, lane >= SOURCES

    def up_z(v):
        return jnp.where(not_last, pltpu.roll(v, LANES - SOURCES, 1), 0.0)

    def down_z(v):
        return jnp.where(not_first, pltpu.roll(v, SOURCES, 1), 0.0)

    def new_h(n, i):
        p, q = i & (PX - 1), (i + 1) & (PX - 1)
        e_x, e_y, e_z = ee[n, 0, p], ee[n, 1, p], ee[n, 2, p]
        e_yn, e_zn = ee[n, 1, q], ee[n, 2, q]
        h_x = hh[0, p] - TIME_STEP * ((pltpu.roll(e_z, PY - 1, 0) - e_z) - (up_z(e_y) - e_y))
        h_y = hh[1, p] - TIME_STEP * ((up_z(e_x) - e_x) - (e_zn - e_z))
        h_z = hh[2, p] - TIME_STEP * ((e_yn - e_y) - (pltpu.roll(e_x, PY - 1, 0) - e_x))
        hh[0, p], hh[1, p], hh[2, p] = h_x, h_y, h_z
        return h_x, h_y, h_z

    def new_e(n, i, h, h_before):
        p = i & (PX - 1)
        h_x, h_y, h_z = h
        h_yb, h_zb = h_before
        s = ss[p]
        e_x = ee[n, 0, p] + s * ((h_z - pltpu.roll(h_z, 1, 0)) - (h_y - down_z(h_y)))
        e_y = ee[n, 1, p] + s * ((h_x - down_z(h_x)) - (h_z - h_zb))
        e_z = ee[n, 2, p] + s * ((h_y - h_yb) - (h_x - pltpu.roll(h_x, 1, 0)))
        ee[n + 1, 0, p], ee[n + 1, 1, p], ee[n + 1, 2, p] = e_x, e_y, e_z

    for n in range(ITERS):
        left, right = -(HALO - n), BX + HALO - 1 - n
        h = new_h(n, jnp.int32(left))

        def plane(i, before, n=n):
            h = new_h(n, i)
            new_e(n, i, h, before)
            return h[1], h[2]

        lax.fori_loop(left + 1, right, plane, (h[1], h[2]), unroll=True)

    own = (slice(None), pl.ds(0, BX), pl.ds(0, BY))
    copies = [
        pltpu.make_async_copy(ee.at[(ITERS,) + own], e_out, sems.at[0]),
        pltpu.make_async_copy(hh.at[own], h_out, sems.at[1]),
    ]
    for copy in copies:
        copy.start()

    even_lane = iota((BY, LANES), 1) % 2 == 0

    def gram(j, sums):
        c, p = j // BX, j % BX
        e = [ee[n + 1, c, p, pl.ds(0, BY)] for n in range(ITERS)]
        permit = permit_ref[p]
        f = [sum(w_ref[n, k] * e[n] for n in range(ITERS)) for k in range(FILTERS)]
        g = [v * permit for v in f]
        o = [jnp.where(even_lane, pltpu.roll(v, LANES - 1, 1), pltpu.roll(v, 1, 1)) for v in g]
        new = []
        for right in (g, o):
            for k in range(FILTERS):
                for l in range(k, FILTERS):
                    v = f[k] * right[l]
                    new.append(v[:8] + v[8:])
        return tuple(s + v for s, v in zip(sums, new))

    zero = jnp.zeros((8, LANES), jnp.float32)
    sums = lax.fori_loop(0, 3 * BX, gram, (zero,) * 20, unroll=4)
    row_of = iota((32, LANES), 0)
    rows = jnp.zeros((32, LANES), jnp.float32)
    at = 0
    for cross in range(2):
        for k in range(FILTERS):
            for l in range(k, FILTERS):
                line = jnp.sum(sums[at], axis=0, keepdims=True)
                rows = jnp.where(row_of == cross * 16 + k * 4 + l, line, rows)
                at += 1

    def entry(shape):
        j = iota(shape, 1)
        k, s, l, t = (j >> 4) & 3, (j >> 3) & 1, (j >> 1) & 3, j & 1
        source = jnp.where(k <= l, s, t)
        which = jnp.where(s == t, 0, 16) + jnp.minimum(k, l) * 4 + jnp.maximum(k, l)
        return jnp.where(j < 64, which, -1), source

    lane_source = (iota((LANES, LANES), 0) & 1 == entry((LANES, LANES))[1]).astype(jnp.float32)
    totals = jnp.dot(rows, lane_source, precision=lax.Precision.HIGHEST, preferred_element_type=jnp.float32)
    vector = jnp.sum(jnp.where(row_of == entry((32, LANES))[0], totals, 0.0), axis=0, keepdims=True)
    part_ref[...] = jnp.broadcast_to(vector[None], part_ref.shape)
    for copy in copies:
        copy.wait()


def add_up(in_ref, out_ref):
    out_ref[...] = jnp.broadcast_to(jnp.sum(in_ref[...], axis=0, keepdims=True), out_ref.shape)


def finish(cells, in_ref, out_ref):
    vector = jnp.broadcast_to(jnp.sum(in_ref[...], axis=0), (8, LANES))
    picked = jnp.where(iota((8, LANES), 1) // 8 == iota((8, LANES), 0), vector, 0.0)
    fold = (iota((LANES, LANES), 0) % 8 == iota((LANES, LANES), 1)).astype(jnp.float32)
    total = jnp.dot(picked, fold, precision=lax.Precision.HIGHEST, preferred_element_type=jnp.float32)
    out_ref[...] = total[:, :8] / cells


def swap_pairs(count, odd, wrap=True):
    if not odd:
        return [(i, i ^ 1) for i in range(count)]
    inner = range(count) if wrap else range(1, count - 1)
    return [(i, (i + 1) % count if i % 2 else (i - 1) % count) for i in inner]


def sum_groups(n_gx, n_gy):
    planes, columns = {}, {}
    for gx in range(n_gx):
        for gy in range(n_gy):
            y, z_high, x = gx // 8, (gx // 4) % 2, gx % 4
            z, core = z_high * 8 + gy // 2, gy % 2
            planes.setdefault(z, []).append(gx * n_gy + gy)
            columns.setdefault((x, y, core), []).append(gx * n_gy + gy)
    return list(planes.values()), list(columns.values())


def body(e_field, h_field, material, permittivity, frequencies):
    n_gx, n_gy = lax.axis_size("gx"), lax.axis_size("gy")
    weights = jnp.cos(frequencies[None, :] * (jnp.arange(1, ITERS + 1, dtype=jnp.float32)[:, None] * TIME_STEP))
    x_message = (f32(XTILES * 8, LANES),) * 2
    y_first = (f32(7 * (BX + HALO) // 2, 8, LANES),) * 2
    y_corner = f32(7 * HALO // 2, 8, LANES)
    scratch = (pltpu.VMEM((2, 3, BY, NZ), jnp.int32), pltpu.SemaphoreType.DMA((2, 7)))
    send_a, send_b = call(pack_x, x_message, "pack_x", 3, scratch=scratch, hbm=(0, 1, 2), size=1 << 20)(
        *(
            pltpu.with_memory_space_constraint(v, pltpu.HBM)
            for v in (e_field.reshape(3, BX * BY, LANES), h_field.reshape(3, BX * BY, LANES), material)
        )
    )
    got_a = lax.ppermute(send_a, "gx", swap_pairs(n_gx, False))
    got_b = lax.ppermute(send_b, "gx", swap_pairs(n_gx, True))
    permit, scaled = call(own_cells, (f32(BX, BY, LANES),) * 2, "own_cells", 2, smem=(1,), size=1 << 18)(
        material, permittivity
    )
    ghosts = (f32(3, HALO, BY, LANES), f32(3, HALO, BY, LANES), f32(HALO, BY, LANES))
    *near, send_a, send_b, send_c = call(near_side, ghosts + y_first + (y_corner,), "near_side", 5, smem=(4,), size=1 << 20)(
        e_field, h_field, scaled, got_a, permittivity
    )
    end = n_gy - 1
    diagonal = [(a * n_gy + g, b * n_gy + end - g) for a, b in swap_pairs(n_gx, True) for g in (0, end)]
    yb1 = lax.ppermute(send_b, "gy", swap_pairs(n_gy, True))
    corner = lax.ppermute(send_c, ("gx", "gy"), diagonal)
    ya1 = lax.ppermute(send_a, "gy", swap_pairs(n_gy, False))
    got_b, ya1 = lax.optimization_barrier((got_b, ya1))
    *far, send_a, send_b = call(far_side, ghosts + (y_corner, y_corner), "far_side", 2, smem=(1,), size=1 << 20)(
        got_b, permittivity
    )
    ya2 = lax.ppermute(send_a, "gy", swap_pairs(n_gy, False))
    yb2 = lax.ppermute(send_b, "gy", swap_pairs(n_gy, True, wrap=False))
    planes, columns = sum_groups(n_gx, n_gy)
    n_plane, n_column = len(planes[0]), len(columns[0])
    scratch = (
        pltpu.VMEM((ITERS + 1, 3, PX, PY, LANES), jnp.float32),
        pltpu.VMEM((3, PX, PY, LANES), jnp.float32),
        pltpu.VMEM((PX, PY, LANES), jnp.float32),
        pltpu.SemaphoreType.DMA((2,)),
    )
    outs = (f32(3, BX, BY, LANES), f32(3, BX, BY, LANES), f32(n_plane, 1, LANES))
    e_out, h_out, part = call(
        steps, outs, "steps", 16, scratch=scratch, smem=(15,), hbm_out=(0, 1), flops=1 << 24, size=1 << 22
    )(e_field, h_field, scaled, permit, *near, *far, ya1, yb1, ya2, yb2, corner, weights)
    both = ("gx", "gy")
    part = lax.all_to_all(part, both, 0, 0, axis_index_groups=planes, tiled=True)
    part = call(add_up, f32(n_column, 1, LANES), "add_up", 1, size=1 << 14)(part)
    part = lax.all_to_all(part, both, 0, 0, axis_index_groups=columns, tiled=True)
    cells = float(BX * n_gx * BY * n_gy * NZ)

    def last(in_ref, out_ref):
        finish(cells, in_ref, out_ref)

    gram = call(last, f32(8, 8), "finish", 1, size=1 << 14)(part)
    return e_out, h_out, gram


def solution(mesh):
    in_specs = (P(None, "gx", "gy", None), P(None, "gx", "gy", None), P("gx", "gy", None), P(), P())
    out_specs = (P(None, "gx", "gy", None), P(None, "gx", "gy", None), P())
    return jax.shard_map(body, mesh=mesh, in_specs=in_specs, out_specs=out_specs, check_vma=False)
```

```python
import jax
import jax.numpy as jnp
from jax import lax
from jax.experimental import pallas as pl
from jax.experimental.pallas import tpu as pltpu
from jax.sharding import PartitionSpec as P

NZ = 64
SOURCES = 2
FILTERS = 4
MATERIALS = 4
ITERS = 4
TIME_STEP = 0.5

BX, BY, LANES = 8, 16, NZ * SOURCES
HALO = ITERS
PX = BX + 2 * HALO
PY = BY + 2 * HALO
XTILES = 49

VMEM = pl.BlockSpec(memory_space=pltpu.VMEM)
HBM = pl.BlockSpec(memory_space=pltpu.HBM)
SMEM = pl.BlockSpec(memory_space=pltpu.SMEM)
PARAMS = pltpu.CompilerParams(vmem_limit_bytes=32 * 1024 * 1024)


def iota(shape, dim):
    return lax.broadcasted_iota(jnp.int32, shape, dim)


def call(kernel, outs, name, n_in, scratch=(), smem=(), hbm=(), hbm_out=(), flops=0, size=0):
    out_specs = tuple(HBM if i in hbm_out else VMEM for i in range(len(outs))) if isinstance(outs, tuple) else VMEM
    return pl.pallas_call(
        kernel,
        out_shape=outs,
        in_specs=[SMEM if i in smem else HBM if i in hbm else VMEM for i in range(n_in)],
        out_specs=out_specs,
        scratch_shapes=list(scratch),
        compiler_params=PARAMS,
        cost_estimate=pl.CostEstimate(flops=flops, bytes_accessed=size, transcendentals=0),
        name=name,
    )


def f32(*shape):
    return jax.ShapeDtypeStruct(shape, jnp.float32)


def x_parts(e, h, wide, narrow):
    return ((e, 0, 4, wide), (e, 1, 4, wide), (e, 2, 4, wide), (h, 0, 3, narrow), (h, 1, 4, wide), (h, 2, 4, wide))


def pack_x(e_ref, h_ref, m_ref, a_ref, b_ref, edge, sems):
    even = lax.rem(lax.axis_index("gx"), 2) == 0
    copies = []
    for side, (out, upper) in enumerate(((a_ref, even), (b_ref, jnp.logical_not(even)))):
        wide = jnp.where(upper, BX - HALO, 0)
        narrow = jnp.where(upper, BX - HALO + 1, 0)
        copies.append(pltpu.make_async_copy(m_ref.at[pl.ds(narrow, 3)], edge.at[side], sems.at[side, 6]))
        row = 0
        for i, (ref, c, n, start) in enumerate(x_parts(e_ref, h_ref, wide, narrow)):
            src = ref.at[c, pl.ds(pl.multiple_of(start * BY, BY), n * BY)]
            copies.append(pltpu.make_async_copy(src, out.at[pl.ds(row, n * BY)], sems.at[side, i]))
            row += n * BY
    for copy in copies:
        copy.start()
    r, col = iota((NZ, LANES), 0), iota((NZ, LANES), 1)
    low = (col == r).astype(jnp.bfloat16)
    high = (col == r + NZ).astype(jnp.bfloat16)
    for side, out in enumerate((a_ref, b_ref)):
        copies[7 * side].wait()
        for i in range(3):
            cells = edge[side, i].astype(jnp.float32).astype(jnp.bfloat16)
            out[pl.ds(8 * (XTILES - 3 + i), 8)] = jnp.dot(
                cells[:8], low, preferred_element_type=jnp.float32
            ) + jnp.dot(cells[8:], high, preferred_element_type=jnp.float32)
    for i, copy in enumerate(copies):
        if i % 7:
            copy.wait()


def look_up(index, table_ref):
    value = jnp.full(index.shape, table_ref[0], jnp.float32)
    for m in range(1, MATERIALS):
        value = jnp.where(index == float(m), table_ref[m], value)
    return value


def spread(rows, offset):
    shape = (rows, LANES)
    return (iota(shape, 1) // SOURCES + offset == iota(shape, 0)).astype(jnp.bfloat16)


def own_block(e_in, h_in, m_in, p_ref, e_ref, h_ref, permit_ref, scaled_ref, cells, sems):
    ends = ((e_in, e_ref), (h_in, h_ref), (m_in, cells))
    copies = [pltpu.make_async_copy(src, dst, sems.at[i]) for i, (src, dst) in enumerate(ends)]
    for copy in copies:
        copy.start()
    copies[2].wait()
    index = cells[...].reshape(BX * BY, NZ).astype(jnp.float32).astype(jnp.bfloat16)
    permit = look_up(jnp.dot(index, spread(NZ, 0), preferred_element_type=jnp.float32), p_ref)
    permit_ref[...] = permit.reshape(BX, BY, LANES)
    scaled_ref[...] = (TIME_STEP / permit).reshape(BX, BY, LANES)
    for copy in copies[:2]:
        copy.wait()


def fill_ghosts(src, after, p_ref, e_ref, h_ref, s_ref):
    narrow = jnp.where(after, 0, 1)
    row = 0
    for ref, c, n, start in x_parts(e_ref, h_ref, 0, narrow):
        ref[c, pl.ds(start, n)] = src[pl.ds(row, n * BY)].reshape(n, BY, LANES)
        row += n * BY
    cells = src[pl.ds(row, 24)].astype(jnp.bfloat16)
    for half in range(2):
        index = jnp.dot(cells, spread(LANES, half * NZ), preferred_element_type=jnp.float32)
        value = TIME_STEP / look_up(index, p_ref)
        for i in range(3):
            s_ref[narrow + i, pl.ds(8 * half, 8)] = value[8 * i : 8 * i + 8]
    unused = jnp.where(after, 3, 0)
    h_ref[0, unused] = jnp.zeros((BY, LANES), jnp.float32)
    s_ref[unused] = jnp.zeros((BY, LANES), jnp.float32)


def edge_rows(ref, low, high):
    first = iota((8, LANES), 0) < HALO
    top = jnp.where(first, pltpu.roll(ref[low, 8:16], HALO, 0), ref[high, 8:16])
    bottom = jnp.where(first, ref[low, 0:8], pltpu.roll(ref[high, 0:8], HALO, 0))
    return top, bottom


def pack_y(parts, ya_ref, yb_ref):
    even = lax.rem(lax.axis_index("gy"), 2) == 0
    for tile, (ref, low, high) in enumerate(parts):
        top, bottom = edge_rows(ref, low, high)
        ya_ref[tile] = jnp.where(even, top, bottom)
        yb_ref[tile] = jnp.where(even, bottom, top)


def unpack_y(parts, ya_ref, yb_ref, other=None):
    even = lax.rem(lax.axis_index("gy"), 2) == 0
    wraps = lax.rem(lax.axis_index("gy") + 1, lax.axis_size("gy")) < 2
    first = iota((8, LANES), 0) < HALO
    for tile, (ref, low, high) in enumerate(parts):
        a, b = ya_ref[tile], yb_ref[tile]
        if other is not None:
            b = jnp.where(wraps, other[tile], b)
        after, before = jnp.where(even, a, b), jnp.where(even, b, a)
        ref[low, BY:PY] = jnp.where(first, after, pltpu.roll(before, HALO, 0))
        ref[high, BY:PY] = jnp.where(first, pltpu.roll(after, HALO, 0), before)


def fields(e, h, s):
    return [e.at[c] for c in range(3)] + [h.at[c] for c in range(3)] + [s]


def pairs_of(refs, planes, base=0):
    return [(ref, base + p, base + p + planes // 2) for ref in refs for p in range(planes // 2)]


def near_side(e_ref, h_ref, s_ref, a_ref, p_ref, ge_ref, gh_ref, gs_ref, ya_ref, yb_ref, corner_ref):
    even = lax.rem(lax.axis_index("gx"), 2) == 0
    fill_ghosts(a_ref, even, p_ref, ge_ref, gh_ref, gs_ref)
    own = fields(e_ref, h_ref, s_ref)
    pack_y(pairs_of(own, BX) + pairs_of(fields(ge_ref, gh_ref, gs_ref), HALO), ya_ref, yb_ref)
    start = jnp.where(even, 0, BX - HALO)
    upper = lax.rem(lax.axis_index("gy"), 2) == 1
    for tile, (ref, low, high) in enumerate(pairs_of(own, HALO, start)):
        top, bottom = edge_rows(ref, low, high)
        corner_ref[tile] = jnp.where(upper, top, bottom)


def far_side(b_ref, p_ref, ge_ref, gh_ref, gs_ref, ya_ref, yb_ref):
    odd = lax.rem(lax.axis_index("gx"), 2) == 1
    fill_ghosts(b_ref, odd, p_ref, ge_ref, gh_ref, gs_ref)
    pack_y(pairs_of(fields(ge_ref, gh_ref, gs_ref), HALO), ya_ref, yb_ref)


def up_z(v):
    return jnp.where(iota(v.shape, 1) < LANES - SOURCES, pltpu.roll(v, LANES - SOURCES, 1), 0.0)


def down_z(v):
    return jnp.where(iota(v.shape, 1) >= SOURCES, pltpu.roll(v, SOURCES, 1), 0.0)


def next_y(v):
    return pltpu.roll(v, PY - 1, 0)


def prev_y(v):
    return pltpu.roll(v, 1, 0)


def advance(h_planes, e_planes, e_at, h_at, scale_at, put_e, put_h):
    fresh = {}

    def new_h(c, i):
        return fresh[i][c] if i in fresh else h_at(c, i)

    for i in sorted({*h_planes, *e_planes}):
        e_x, e_y, e_z = (e_at(c, i) for c in range(3))
        if i in h_planes:
            e_yn, e_zn = e_at(1, i + 1), e_at(2, i + 1)
            h_x = h_at(0, i) - TIME_STEP * ((next_y(e_z) - e_z) - (up_z(e_y) - e_y))
            h_y = h_at(1, i) - TIME_STEP * ((up_z(e_x) - e_x) - (e_zn - e_z))
            h_z = h_at(2, i) - TIME_STEP * ((e_yn - e_y) - (next_y(e_x) - e_x))
            fresh[i] = (h_x, h_y, h_z)
            put_h(i, fresh[i])
        if i in e_planes:
            h_x, h_y, h_z = (new_h(c, i) for c in range(3))
            h_yb, h_zb = new_h(1, i - 1), new_h(2, i - 1)
            s = scale_at(i)
            e_x = e_x + s * ((h_z - prev_y(h_z)) - (h_y - down_z(h_y)))
            e_y = e_y + s * ((h_x - down_z(h_x)) - (h_z - h_zb))
            e_z = e_z + s * ((h_y - h_yb) - (h_x - prev_y(h_x)))
            put_e(i, (e_x, e_y, e_z))


def gram_terms(e_at, permit_ref, w_ref, planes, sums):
    even_lane = iota((BY, LANES), 1) % 2 == 0
    for i in planes:
        permit = permit_ref[i]
        for c in range(3):
            e = [e_at(n, c, i)[:BY] for n in range(1, ITERS + 1)]
            f = [sum(w_ref[n, k] * e[n] for n in range(ITERS)) for k in range(FILTERS)]
            g = [v * permit for v in f]
            o = [jnp.where(even_lane, pltpu.roll(v, LANES - 1, 1), pltpu.roll(v, 1, 1)) for v in g]
            at = 0
            sums = list(sums)
            for right in (g, o):
                for k in range(FILTERS):
                    for l in range(k, FILTERS):
                        v = f[k] * right[l]
                        sums[at] = sums[at] + (v[:8] + v[8:])
                        at += 1
    return sums


def both_sides(act):
    even = lax.rem(lax.axis_index("gx"), 2) == 0
    pl.when(even)(lambda: act(True))
    pl.when(jnp.logical_not(even))(lambda: act(False))


def near_h(before, n):
    return range(n - 1, BX + HALO - n) if before else range(n - 1 - HALO, BX - n)


def near_e(before, n):
    if n == 0:
        return range(0, BX + HALO) if before else range(-HALO, BX)
    return range(n, BX + HALO - n) if before else range(n - HALO, BX - n)


def near_planes(before):
    near = range(HALO, BX) if before else range(0, BX - HALO)
    return near, [i for i in range(BX) if i not in near]


def near_steps(own_e, own_h, own_s, permit_ref, ge, gh, gs, ya1, yb1, w_ref, ee, hh, ss, sums_ref):
    def act(before):
        base = BX if before else BX + HALO
        extended = fields(ee.at[0], hh, ss)
        for dst, own, ghost in zip(extended, fields(own_e, own_h, own_s), fields(ge, gh, gs)):
            dst[:BX, :BY] = own[...]
            dst[base : base + HALO, :BY] = ghost[...]
        unpack_y(pairs_of(extended, BX) + pairs_of(extended, HALO, base), ya1, yb1)

        def put_h(i, values):
            for c in range(3):
                hh[c, i % PX] = values[c]

        for n in range(1, ITERS + 1):

            def put_e(i, values, n=n):
                for c in range(3):
                    ee[n, c, i % PX] = values[c]

            advance(
                near_h(before, n), near_e(before, n),
                lambda c, i: ee[n - 1, c, i % PX], lambda c, i: hh[c, i % PX], lambda i: ss[i % PX], put_e, put_h,
            )
        sums = gram_terms(
            lambda n, c, i: ee[n, c, i], permit_ref, w_ref, near_planes(before)[0], [jnp.zeros((8, LANES), jnp.float32)] * 20
        )
        for i in range(20):
            sums_ref[i] = sums[i]

    both_sides(act)


def far_steps(
    ee, hh, ss, sums_in, permit_ref, ge, gh, gs, corner, yb2, ya2, w_ref, e_out, h_out, part_ref, fe, fh, fs, sums_ref, sems
):
    def act(before):
        base = BX + HALO if before else BX
        near, rest = near_planes(before)
        near_h_out = [i for i in range(BX) if i in near_h(before, ITERS)]
        rest_h_out = [i for i in range(BX) if i not in near_h_out]

        def copies_of(which, e, h, e_planes, h_planes):
            e_at, h_at = pl.ds(e_planes[0], len(e_planes)), pl.ds(h_planes[0], len(h_planes))
            return [
                pltpu.make_async_copy(e.at[ITERS, :, e_at, pl.ds(0, BY)], e_out.at[:, e_at], sems.at[which, 0]),
                pltpu.make_async_copy(h.at[:, h_at, pl.ds(0, BY)], h_out.at[:, h_at], sems.at[which, 1]),
            ]

        copies = copies_of(0, ee, hh, near, near_h_out)
        for copy in copies:
            copy.start()
        extended = fields(fe.at[0], fh, fs)
        for dst, ghost in zip(extended, fields(ge, gh, gs)):
            dst[base : base + HALO, :BY] = ghost[...]
        unpack_y(pairs_of(extended, HALO, base), ya2, yb2, corner)
        done = set()
        far = range(-HALO, 0) if before else range(BX, BX + HALO)

        def e_at(n, c, i):
            return (ee if i in near_e(before, n) else fe)[n, c, i % PX]

        def h_at(c, i):
            return (fh if i in done or i in far else hh)[c, i % PX]

        def scale_at(i):
            return (fs if i in far else ss)[i % PX]

        def put_h(i, values):
            done.add(i)
            for c in range(3):
                fh[c, i % PX] = values[c]

        for n in range(1, ITERS + 1):

            def put_e(i, values, n=n):
                for c in range(3):
                    fe[n, c, i % PX] = values[c]

            all_h = range(n - 1 - HALO, BX + HALO - n)
            all_e = range(n - HALO, BX + HALO - n)
            advance(
                [i for i in all_h if i not in near_h(before, n)], [i for i in all_e if i not in near_e(before, n)],
                lambda c, i: e_at(n - 1, c, i), h_at, scale_at, put_e, put_h,
            )
        last = copies_of(1, fe, fh, rest, rest_h_out)
        for copy in last:
            copy.start()
        sums = gram_terms(e_at, permit_ref, w_ref, rest, [sums_in[i] for i in range(20)])
        for i in range(20):
            sums_ref[i] = sums[i]
        for copy in copies + last:
            copy.wait()

    both_sides(act)
    row_of = iota((32, LANES), 0)
    rows = jnp.zeros((32, LANES), jnp.float32)
    at = 0
    for cross in range(2):
        for k in range(FILTERS):
            for l in range(k, FILTERS):
                line = jnp.sum(sums_ref[at], axis=0, keepdims=True)
                rows = jnp.where(row_of == cross * 16 + k * 4 + l, line, rows)
                at += 1

    def entry(shape):
        j = iota(shape, 1)
        k, s, l, t = (j >> 4) & 3, (j >> 3) & 1, (j >> 1) & 3, j & 1
        source = jnp.where(k <= l, s, t)
        which = jnp.where(s == t, 0, 16) + jnp.minimum(k, l) * 4 + jnp.maximum(k, l)
        return jnp.where(j < 64, which, -1), source

    lane_source = (iota((LANES, LANES), 0) & 1 == entry((LANES, LANES))[1]).astype(jnp.float32)
    totals = jnp.dot(rows, lane_source, precision=lax.Precision.HIGHEST, preferred_element_type=jnp.float32)
    vector = jnp.sum(jnp.where(row_of == entry((32, LANES))[0], totals, 0.0), axis=0, keepdims=True)
    part_ref[...] = jnp.broadcast_to(vector[None], part_ref.shape)


def add_up(in_ref, out_ref):
    out_ref[...] = jnp.broadcast_to(jnp.sum(in_ref[...], axis=0, keepdims=True), out_ref.shape)


def finish(cells, in_ref, out_ref):
    vector = jnp.broadcast_to(jnp.sum(in_ref[...], axis=0), (8, LANES))
    picked = jnp.where(iota((8, LANES), 1) // 8 == iota((8, LANES), 0), vector, 0.0)
    fold = (iota((LANES, LANES), 0) % 8 == iota((LANES, LANES), 1)).astype(jnp.float32)
    total = jnp.dot(picked, fold, precision=lax.Precision.HIGHEST, preferred_element_type=jnp.float32)
    out_ref[...] = total[:, :8] / cells


def swap_pairs(count, odd, wrap=True):
    if not odd:
        return [(i, i ^ 1) for i in range(count)]
    inner = range(count) if wrap else range(1, count - 1)
    return [(i, (i + 1) % count if i % 2 else (i - 1) % count) for i in inner]


def sum_groups(n_gx, n_gy):
    planes, columns = {}, {}
    for gx in range(n_gx):
        for gy in range(n_gy):
            y, z_high, x = gx // 8, (gx // 4) % 2, gx % 4
            z, core = z_high * 8 + gy // 2, gy % 2
            planes.setdefault(z, []).append(gx * n_gy + gy)
            columns.setdefault((x, y, core), []).append(gx * n_gy + gy)
    return list(planes.values()), list(columns.values())


def body(e_field, h_field, material, permittivity, frequencies):
    n_gx, n_gy = lax.axis_size("gx"), lax.axis_size("gy")
    weights = jnp.cos(frequencies[None, :] * (jnp.arange(1, ITERS + 1, dtype=jnp.float32)[:, None] * TIME_STEP))
    x_message = (f32(XTILES * 8, LANES),) * 2
    y_first = (f32(7 * (BX + HALO) // 2, 8, LANES),) * 2
    y_corner = f32(7 * HALO // 2, 8, LANES)
    scratch = (pltpu.VMEM((2, 3, BY, NZ), jnp.int32), pltpu.SemaphoreType.DMA((2, 7)))
    block = [
        pltpu.with_memory_space_constraint(v, pltpu.HBM)
        for v in (e_field.reshape(3, BX * BY, LANES), h_field.reshape(3, BX * BY, LANES), material)
    ]
    send_a, send_b = call(pack_x, x_message, "pack_x", 3, scratch=scratch, hbm=(0, 1, 2), size=1 << 20)(*block)
    got_a = lax.ppermute(send_a, "gx", swap_pairs(n_gx, False))
    got_b = lax.ppermute(send_b, "gx", swap_pairs(n_gx, True))
    outs = (f32(3, BX * BY, LANES), f32(3, BX * BY, LANES), f32(BX, BY, LANES), f32(BX, BY, LANES))
    scratch = (pltpu.VMEM((BX, BY, NZ), jnp.int32), pltpu.SemaphoreType.DMA((3,)))
    permittivity, weights = lax.optimization_barrier((permittivity, weights))
    own_e, own_h, permit, scaled = call(
        own_block, outs, "own_block", 4, scratch=scratch, smem=(3,), hbm=(0, 1, 2), size=1 << 20
    )(*block, permittivity)
    own_e, own_h = own_e.reshape(e_field.shape), own_h.reshape(h_field.shape)
    ghosts = (f32(3, HALO, BY, LANES), f32(3, HALO, BY, LANES), f32(HALO, BY, LANES))
    *near, send_a, send_b, send_c = call(near_side, ghosts + y_first + (y_corner,), "near_side", 5, smem=(4,), size=1 << 20)(
        own_e, own_h, scaled, got_a, permittivity
    )
    end = n_gy - 1
    diagonal = [(a * n_gy + g, b * n_gy + end - g) for a, b in swap_pairs(n_gx, True) for g in (0, end)]
    yb1 = lax.ppermute(send_b, "gy", swap_pairs(n_gy, True))
    corner = lax.ppermute(send_c, ("gx", "gy"), diagonal)
    ya1 = lax.ppermute(send_a, "gy", swap_pairs(n_gy, False))
    got_b, ya1 = lax.optimization_barrier((got_b, ya1))
    *far, send_a, send_b = call(far_side, ghosts + (y_corner, y_corner), "far_side", 2, smem=(1,), size=1 << 20)(
        got_b, permittivity
    )
    ya2 = lax.ppermute(send_a, "gy", swap_pairs(n_gy, False))
    yb2 = lax.ppermute(send_b, "gy", swap_pairs(n_gy, True, wrap=False))
    planes, columns = sum_groups(n_gx, n_gy)
    n_plane, n_column = len(planes[0]), len(columns[0])
    levels = (f32(ITERS + 1, 3, PX, PY, LANES), f32(3, PX, PY, LANES), f32(PX, PY, LANES))
    sums = f32(20, 8, LANES)
    state = call(near_steps, levels + (sums,), "near_steps", 10, smem=(9,), flops=1 << 24, size=1 << 22)(
        own_e, own_h, scaled, permit, *near, ya1, yb1, weights
    )
    scratch = [pltpu.VMEM(v.shape, jnp.float32) for v in levels + (sums,)] + [pltpu.SemaphoreType.DMA((2, 2))]
    outs = (f32(3, BX, BY, LANES), f32(3, BX, BY, LANES), f32(n_plane, 1, LANES))
    e_out, h_out, part = call(
        far_steps, outs, "far_steps", 12, scratch=scratch, smem=(11,), hbm_out=(0, 1), flops=1 << 24, size=1 << 22
    )(*state, permit, *far, corner, yb2, ya2, weights)
    both = ("gx", "gy")
    part = lax.all_to_all(part, both, 0, 0, axis_index_groups=planes, tiled=True)
    part = call(add_up, f32(n_column, 1, LANES), "add_up", 1, size=1 << 14)(part)
    part = lax.all_to_all(part, both, 0, 0, axis_index_groups=columns, tiled=True)
    cells = float(BX * n_gx * BY * n_gy * NZ)

    def last(in_ref, out_ref):
        finish(cells, in_ref, out_ref)

    gram = call(last, f32(8, 8), "finish", 1, size=1 << 14)(part)
    return e_out, h_out, gram


def solution(mesh):
    in_specs = (P(None, "gx", "gy", None), P(None, "gx", "gy", None), P("gx", "gy", None), P(), P())
    out_specs = (P(None, "gx", "gy", None), P(None, "gx", "gy", None), P())
    return jax.shard_map(body, mesh=mesh, in_specs=in_specs, out_specs=out_specs, check_vma=False)
```

```python
import jax
import jax.numpy as jnp
from jax import lax
from jax.experimental import pallas as pl
from jax.experimental.pallas import tpu as pltpu
from jax.sharding import PartitionSpec as P

NZ = 64
SOURCES = 2
FILTERS = 4
MATERIALS = 4
ITERS = 4
TIME_STEP = 0.5

BX, BY, LANES = 8, 16, NZ * SOURCES
HALO = ITERS
PX = BX + 2 * HALO
PY = BY + 2 * HALO
XTILES = 49

VMEM = pl.BlockSpec(memory_space=pltpu.VMEM)
HBM = pl.BlockSpec(memory_space=pltpu.HBM)
SMEM = pl.BlockSpec(memory_space=pltpu.SMEM)
PARAMS = pltpu.CompilerParams(vmem_limit_bytes=32 * 1024 * 1024)


def iota(shape, dim):
    return lax.broadcasted_iota(jnp.int32, shape, dim)


def call(kernel, outs, name, n_in, scratch=(), smem=(), hbm=(), hbm_out=(), flops=0, size=0):
    out_specs = tuple(HBM if i in hbm_out else VMEM for i in range(len(outs))) if isinstance(outs, tuple) else VMEM
    return pl.pallas_call(
        kernel,
        out_shape=outs,
        in_specs=[SMEM if i in smem else HBM if i in hbm else VMEM for i in range(n_in)],
        out_specs=out_specs,
        scratch_shapes=list(scratch),
        compiler_params=PARAMS,
        cost_estimate=pl.CostEstimate(flops=flops, bytes_accessed=size, transcendentals=0),
        name=name,
    )


def f32(*shape):
    return jax.ShapeDtypeStruct(shape, jnp.float32)


def x_parts(e, h, wide, narrow):
    return ((e, 0, 4, wide), (e, 1, 4, wide), (e, 2, 4, wide), (h, 0, 3, narrow), (h, 1, 4, wide), (h, 2, 4, wide))


def pack_x(e_ref, h_ref, m_ref, a_ref, b_ref, edge, sems):
    even = lax.rem(lax.axis_index("gx"), 2) == 0
    copies = []
    for side, (out, upper) in enumerate(((a_ref, even), (b_ref, jnp.logical_not(even)))):
        wide = jnp.where(upper, BX - HALO, 0)
        narrow = jnp.where(upper, BX - HALO + 1, 0)
        copies.append(pltpu.make_async_copy(m_ref.at[pl.ds(narrow, 3)], edge.at[side], sems.at[side, 6]))
        row = 0
        for i, (ref, c, n, start) in enumerate(x_parts(e_ref, h_ref, wide, narrow)):
            src = ref.at[c, pl.ds(pl.multiple_of(start * BY, BY), n * BY)]
            copies.append(pltpu.make_async_copy(src, out.at[pl.ds(row, n * BY)], sems.at[side, i]))
            row += n * BY
    for copy in copies:
        copy.start()
    r, col = iota((NZ, LANES), 0), iota((NZ, LANES), 1)
    low = (col == r).astype(jnp.bfloat16)
    high = (col == r + NZ).astype(jnp.bfloat16)
    for side, out in enumerate((a_ref, b_ref)):
        copies[7 * side].wait()
        for i in range(3):
            cells = edge[side, i].astype(jnp.float32).astype(jnp.bfloat16)
            out[pl.ds(8 * (XTILES - 3 + i), 8)] = jnp.dot(
                cells[:8], low, preferred_element_type=jnp.float32
            ) + jnp.dot(cells[8:], high, preferred_element_type=jnp.float32)
    for i, copy in enumerate(copies):
        if i % 7:
            copy.wait()


def look_up(index, table_ref):
    value = jnp.full(index.shape, table_ref[0], jnp.float32)
    for m in range(1, MATERIALS):
        value = jnp.where(index == float(m), table_ref[m], value)
    return value


def spread(rows, offset):
    shape = (rows, LANES)
    return (iota(shape, 1) // SOURCES + offset == iota(shape, 0)).astype(jnp.bfloat16)


def own_block(e_in, h_in, m_in, p_ref, e_ref, h_ref, permit_ref, scaled_ref, cells, sems):
    ends = ((e_in, e_ref), (h_in, h_ref), (m_in, cells))
    copies = [pltpu.make_async_copy(src, dst, sems.at[i]) for i, (src, dst) in enumerate(ends)]
    for copy in copies:
        copy.start()
    copies[2].wait()
    index = cells[...].reshape(BX * BY, NZ).astype(jnp.float32).astype(jnp.bfloat16)
    permit = look_up(jnp.dot(index, spread(NZ, 0), preferred_element_type=jnp.float32), p_ref)
    permit_ref[...] = permit.reshape(BX, BY, LANES)
    scaled_ref[...] = (TIME_STEP / permit).reshape(BX, BY, LANES)
    for copy in copies[:2]:
        copy.wait()


def fill_ghosts(src, after, p_ref, e_ref, h_ref, s_ref, first_row=0):
    narrow = jnp.where(after, 0, 1)
    row = 0
    for ref, c, n, start in x_parts(e_ref, h_ref, 0, narrow):
        ref[c, pl.ds(start, n)] = src[pl.ds(first_row + row, n * BY)].reshape(n, BY, LANES)
        row += n * BY
    cells = src[pl.ds(first_row + row, 24)].astype(jnp.bfloat16)
    for half in range(2):
        index = jnp.dot(cells, spread(LANES, half * NZ), preferred_element_type=jnp.float32)
        value = TIME_STEP / look_up(index, p_ref)
        for i in range(3):
            s_ref[narrow + i, pl.ds(8 * half, 8)] = value[8 * i : 8 * i + 8]
    unused = jnp.where(after, 3, 0)
    h_ref[0, unused] = jnp.zeros((BY, LANES), jnp.float32)
    s_ref[unused] = jnp.zeros((BY, LANES), jnp.float32)


def edge_rows(ref, low, high):
    first = iota((8, LANES), 0) < HALO
    top = jnp.where(first, pltpu.roll(ref[low, 8:16], HALO, 0), ref[high, 8:16])
    bottom = jnp.where(first, ref[low, 0:8], pltpu.roll(ref[high, 0:8], HALO, 0))
    return top, bottom


def pack_y(parts, ya_ref, yb_ref):
    even = lax.rem(lax.axis_index("gy"), 2) == 0
    for tile, (ref, low, high) in enumerate(parts):
        top, bottom = edge_rows(ref, low, high)
        ya_ref[tile] = jnp.where(even, top, bottom)
        yb_ref[tile] = jnp.where(even, bottom, top)


def unpack_y(parts, ya_ref, yb_ref, other=None):
    even = lax.rem(lax.axis_index("gy"), 2) == 0
    wraps = lax.rem(lax.axis_index("gy") + 1, lax.axis_size("gy")) < 2
    first = iota((8, LANES), 0) < HALO
    for tile, (ref, low, high) in enumerate(parts):
        a, b = ya_ref[tile], yb_ref[tile]
        if other is not None:
            b = jnp.where(wraps, other[tile], b)
        after, before = jnp.where(even, a, b), jnp.where(even, b, a)
        ref[low, BY:PY] = jnp.where(first, after, pltpu.roll(before, HALO, 0))
        ref[high, BY:PY] = jnp.where(first, pltpu.roll(after, HALO, 0), before)


def fields(e, h, s):
    return [e.at[c] for c in range(3)] + [h.at[c] for c in range(3)] + [s]


def pairs_of(refs, planes, base=0):
    return [(ref, base + p, base + p + planes // 2) for ref in refs for p in range(planes // 2)]


def near_side(e_ref, h_ref, s_ref, a_ref, p_ref, ge_ref, gh_ref, gs_ref, ya_ref, yb_ref, corner_ref):
    even = lax.rem(lax.axis_index("gx"), 2) == 0
    other = pl.multiple_of(jnp.where(even, 8 * XTILES, 0), 8)
    fill_ghosts(a_ref, even, p_ref, ge_ref, gh_ref, gs_ref, other)
    own = fields(e_ref, h_ref, s_ref)
    pack_y(pairs_of(own, BX) + pairs_of(fields(ge_ref, gh_ref, gs_ref), HALO), ya_ref, yb_ref)
    start = jnp.where(even, 0, BX - HALO)
    upper = lax.rem(lax.axis_index("gy"), 2) == 1
    for tile, (ref, low, high) in enumerate(pairs_of(own, HALO, start)):
        top, bottom = edge_rows(ref, low, high)
        corner_ref[tile] = jnp.where(upper, top, bottom)


def far_side(b_ref, p_ref, ge_ref, gh_ref, gs_ref, ya_ref, yb_ref):
    odd = lax.rem(lax.axis_index("gx"), 2) == 1
    fill_ghosts(b_ref, odd, p_ref, ge_ref, gh_ref, gs_ref)
    pack_y(pairs_of(fields(ge_ref, gh_ref, gs_ref), HALO), ya_ref, yb_ref)


def up_z(v):
    return jnp.where(iota(v.shape, 1) < LANES - SOURCES, pltpu.roll(v, LANES - SOURCES, 1), 0.0)


def down_z(v):
    return jnp.where(iota(v.shape, 1) >= SOURCES, pltpu.roll(v, SOURCES, 1), 0.0)


def next_y(v):
    return pltpu.roll(v, PY - 1, 0)


def prev_y(v):
    return pltpu.roll(v, 1, 0)


def advance(h_planes, e_planes, e_at, h_at, scale_at, put_e, put_h):
    fresh = {}

    def new_h(c, i):
        return fresh[i][c] if i in fresh else h_at(c, i)

    for i in sorted({*h_planes, *e_planes}):
        e_x, e_y, e_z = (e_at(c, i) for c in range(3))
        if i in h_planes:
            e_yn, e_zn = e_at(1, i + 1), e_at(2, i + 1)
            h_x = h_at(0, i) - TIME_STEP * ((next_y(e_z) - e_z) - (up_z(e_y) - e_y))
            h_y = h_at(1, i) - TIME_STEP * ((up_z(e_x) - e_x) - (e_zn - e_z))
            h_z = h_at(2, i) - TIME_STEP * ((e_yn - e_y) - (next_y(e_x) - e_x))
            fresh[i] = (h_x, h_y, h_z)
            put_h(i, fresh[i])
        if i in e_planes:
            h_x, h_y, h_z = (new_h(c, i) for c in range(3))
            h_yb, h_zb = new_h(1, i - 1), new_h(2, i - 1)
            s = scale_at(i)
            e_x = e_x + s * ((h_z - prev_y(h_z)) - (h_y - down_z(h_y)))
            e_y = e_y + s * ((h_x - down_z(h_x)) - (h_z - h_zb))
            e_z = e_z + s * ((h_y - h_yb) - (h_x - prev_y(h_x)))
            put_e(i, (e_x, e_y, e_z))


def gram_terms(e_at, permit_ref, w_ref, planes, sums):
    even_lane = iota((BY, LANES), 1) % 2 == 0
    for i in planes:
        permit = permit_ref[i]
        for c in range(3):
            e = [e_at(n, c, i)[:BY] for n in range(1, ITERS + 1)]
            f = [sum(w_ref[n, k] * e[n] for n in range(ITERS)) for k in range(FILTERS)]
            g = [v * permit for v in f]
            o = [jnp.where(even_lane, pltpu.roll(v, LANES - 1, 1), pltpu.roll(v, 1, 1)) for v in g]
            at = 0
            sums = list(sums)
            for right in (g, o):
                for k in range(FILTERS):
                    for l in range(k, FILTERS):
                        v = f[k] * right[l]
                        sums[at] = sums[at] + (v[:8] + v[8:])
                        at += 1
    return sums


def both_sides(act):
    even = lax.rem(lax.axis_index("gx"), 2) == 0
    pl.when(even)(lambda: act(True))
    pl.when(jnp.logical_not(even))(lambda: act(False))


def near_h(before, n):
    return range(n - 1, BX + HALO - n) if before else range(n - 1 - HALO, BX - n)


def near_e(before, n):
    if n == 0:
        return range(0, BX + HALO) if before else range(-HALO, BX)
    return range(n, BX + HALO - n) if before else range(n - HALO, BX - n)


def near_planes(before):
    near = range(HALO, BX) if before else range(0, BX - HALO)
    return near, [i for i in range(BX) if i not in near]


def near_steps(own_e, own_h, own_s, permit_ref, ge, gh, gs, ya1, yb1, w_ref, ee, hh, ss, sums_ref):
    def act(before):
        base = BX if before else BX + HALO
        extended = fields(ee.at[0], hh, ss)
        for dst, own, ghost in zip(extended, fields(own_e, own_h, own_s), fields(ge, gh, gs)):
            dst[:BX, :BY] = own[...]
            dst[base : base + HALO, :BY] = ghost[...]
        unpack_y(pairs_of(extended, BX) + pairs_of(extended, HALO, base), ya1, yb1)

        def put_h(i, values):
            for c in range(3):
                hh[c, i % PX] = values[c]

        for n in range(1, ITERS + 1):

            def put_e(i, values, n=n):
                for c in range(3):
                    ee[n, c, i % PX] = values[c]

            advance(
                near_h(before, n), near_e(before, n),
                lambda c, i: ee[n - 1, c, i % PX], lambda c, i: hh[c, i % PX], lambda i: ss[i % PX], put_e, put_h,
            )
        sums = gram_terms(
            lambda n, c, i: ee[n, c, i], permit_ref, w_ref, near_planes(before)[0], [jnp.zeros((8, LANES), jnp.float32)] * 20
        )
        for i in range(20):
            sums_ref[i] = sums[i]

    both_sides(act)


def far_steps(
    ee, hh, ss, sums_in, permit_ref, ge, gh, gs, corner, yb2, ya2, w_ref, e_out, h_out, part_ref, fe, fh, fs, sums_ref, sems
):
    def act(before):
        base = BX + HALO if before else BX
        near, rest = near_planes(before)
        near_h_out = [i for i in range(BX) if i in near_h(before, ITERS)]
        rest_h_out = [i for i in range(BX) if i not in near_h_out]

        def copies_of(which, e, h, e_planes, h_planes):
            e_at, h_at = pl.ds(e_planes[0], len(e_planes)), pl.ds(h_planes[0], len(h_planes))
            return [
                pltpu.make_async_copy(e.at[ITERS, :, e_at, pl.ds(0, BY)], e_out.at[:, e_at], sems.at[which, 0]),
                pltpu.make_async_copy(h.at[:, h_at, pl.ds(0, BY)], h_out.at[:, h_at], sems.at[which, 1]),
            ]

        copies = copies_of(0, ee, hh, near, near_h_out)
        for copy in copies:
            copy.start()
        extended = fields(fe.at[0], fh, fs)
        for dst, ghost in zip(extended, fields(ge, gh, gs)):
            dst[base : base + HALO, :BY] = ghost[...]
        unpack_y(pairs_of(extended, HALO, base), ya2, yb2, corner)
        done = set()
        far = range(-HALO, 0) if before else range(BX, BX + HALO)

        def e_at(n, c, i):
            return (ee if i in near_e(before, n) else fe)[n, c, i % PX]

        def h_at(c, i):
            return (fh if i in done or i in far else hh)[c, i % PX]

        def scale_at(i):
            return (fs if i in far else ss)[i % PX]

        def put_h(i, values):
            done.add(i)
            for c in range(3):
                fh[c, i % PX] = values[c]

        for n in range(1, ITERS + 1):

            def put_e(i, values, n=n):
                for c in range(3):
                    fe[n, c, i % PX] = values[c]

            all_h = range(n - 1 - HALO, BX + HALO - n)
            all_e = range(n - HALO, BX + HALO - n)
            advance(
                [i for i in all_h if i not in near_h(before, n)], [i for i in all_e if i not in near_e(before, n)],
                lambda c, i: e_at(n - 1, c, i), h_at, scale_at, put_e, put_h,
            )
        last = copies_of(1, fe, fh, rest, rest_h_out)
        for copy in last:
            copy.start()
        sums = gram_terms(e_at, permit_ref, w_ref, rest, [sums_in[i] for i in range(20)])
        for i in range(20):
            sums_ref[i] = sums[i]
        for copy in copies + last:
            copy.wait()

    both_sides(act)
    row_of = iota((32, LANES), 0)
    rows = jnp.zeros((32, LANES), jnp.float32)
    at = 0
    for cross in range(2):
        for k in range(FILTERS):
            for l in range(k, FILTERS):
                line = jnp.sum(sums_ref[at], axis=0, keepdims=True)
                rows = jnp.where(row_of == cross * 16 + k * 4 + l, line, rows)
                at += 1

    def entry(shape):
        j = iota(shape, 1)
        k, s, l, t = (j >> 4) & 3, (j >> 3) & 1, (j >> 1) & 3, j & 1
        source = jnp.where(k <= l, s, t)
        which = jnp.where(s == t, 0, 16) + jnp.minimum(k, l) * 4 + jnp.maximum(k, l)
        return jnp.where(j < 64, which, -1), source

    lane_source = (iota((LANES, LANES), 0) & 1 == entry((LANES, LANES))[1]).astype(jnp.float32)
    totals = jnp.dot(rows, lane_source, precision=lax.Precision.HIGHEST, preferred_element_type=jnp.float32)
    vector = jnp.sum(jnp.where(row_of == entry((32, LANES))[0], totals, 0.0), axis=0, keepdims=True)
    part_ref[...] = jnp.broadcast_to(vector[None], part_ref.shape)


def add_up(in_ref, out_ref):
    out_ref[...] = jnp.broadcast_to(jnp.sum(in_ref[...], axis=0, keepdims=True), out_ref.shape)


def finish(cells, in_ref, out_ref):
    vector = jnp.broadcast_to(jnp.sum(in_ref[...], axis=0), (8, LANES))
    picked = jnp.where(iota((8, LANES), 1) // 8 == iota((8, LANES), 0), vector, 0.0)
    fold = (iota((LANES, LANES), 0) % 8 == iota((LANES, LANES), 1)).astype(jnp.float32)
    total = jnp.dot(picked, fold, precision=lax.Precision.HIGHEST, preferred_element_type=jnp.float32)
    out_ref[...] = total[:, :8] / cells


def swap_pairs(count, odd, wrap=True):
    if not odd:
        return [(i, i ^ 1) for i in range(count)]
    inner = range(count) if wrap else range(1, count - 1)
    return [(i, (i + 1) % count if i % 2 else (i - 1) % count) for i in inner]


def sum_groups(n_gx, n_gy):
    planes, columns = {}, {}
    for gx in range(n_gx):
        for gy in range(n_gy):
            y, z_high, x = gx // 8, (gx // 4) % 2, gx % 4
            z, core = z_high * 8 + gy // 2, gy % 2
            planes.setdefault(z, []).append(gx * n_gy + gy)
            columns.setdefault((x, y, core), []).append(gx * n_gy + gy)
    return list(planes.values()), list(columns.values())


def body(e_field, h_field, material, permittivity, frequencies):
    n_gx, n_gy = lax.axis_size("gx"), lax.axis_size("gy")
    weights = jnp.cos(frequencies[None, :] * (jnp.arange(1, ITERS + 1, dtype=jnp.float32)[:, None] * TIME_STEP))
    x_message = (f32(XTILES * 8, LANES),) * 2
    y_first = (f32(7 * (BX + HALO) // 2, 8, LANES),) * 2
    y_corner = f32(7 * HALO // 2, 8, LANES)
    scratch = (pltpu.VMEM((2, 3, BY, NZ), jnp.int32), pltpu.SemaphoreType.DMA((2, 7)))
    block = [
        pltpu.with_memory_space_constraint(v, pltpu.HBM)
        for v in (e_field.reshape(3, BX * BY, LANES), h_field.reshape(3, BX * BY, LANES), material)
    ]
    send_a, send_b = call(pack_x, x_message, "pack_x", 3, scratch=scratch, hbm=(0, 1, 2), size=1 << 20)(*block)
    near_pairs = [[i, i + 1] for i in range(0, n_gx, 2)]
    got_a = lax.all_gather(send_a, "gx", axis_index_groups=near_pairs, tiled=True)
    got_b = lax.ppermute(send_b, "gx", swap_pairs(n_gx, True))
    outs = (f32(3, BX * BY, LANES), f32(3, BX * BY, LANES), f32(BX, BY, LANES), f32(BX, BY, LANES))
    scratch = (pltpu.VMEM((BX, BY, NZ), jnp.int32), pltpu.SemaphoreType.DMA((3,)))
    permittivity, weights = lax.optimization_barrier((permittivity, weights))
    own_e, own_h, permit, scaled = call(
        own_block, outs, "own_block", 4, scratch=scratch, smem=(3,), hbm=(0, 1, 2), size=1 << 20
    )(*block, permittivity)
    own_e, own_h = own_e.reshape(e_field.shape), own_h.reshape(h_field.shape)
    ghosts = (f32(3, HALO, BY, LANES), f32(3, HALO, BY, LANES), f32(HALO, BY, LANES))
    *near, send_a, send_b, send_c = call(near_side, ghosts + y_first + (y_corner,), "near_side", 5, smem=(4,), size=1 << 20)(
        own_e, own_h, scaled, got_a, permittivity
    )
    end = n_gy - 1
    diagonal = [(a * n_gy + g, b * n_gy + end - g) for a, b in swap_pairs(n_gx, True) for g in (0, end)]
    yb1 = lax.ppermute(send_b, "gy", swap_pairs(n_gy, True))
    corner = lax.ppermute(send_c, ("gx", "gy"), diagonal)
    ya1 = lax.ppermute(send_a, "gy", swap_pairs(n_gy, False))
    got_b, ya1 = lax.optimization_barrier((got_b, ya1))
    *far, send_a, send_b = call(far_side, ghosts + (y_corner, y_corner), "far_side", 2, smem=(1,), size=1 << 20)(
        got_b, permittivity
    )
    ya2 = lax.ppermute(send_a, "gy", swap_pairs(n_gy, False))
    yb2 = lax.ppermute(send_b, "gy", swap_pairs(n_gy, True, wrap=False))
    planes, columns = sum_groups(n_gx, n_gy)
    n_plane, n_column = len(planes[0]), len(columns[0])
    levels = (f32(ITERS + 1, 3, PX, PY, LANES), f32(3, PX, PY, LANES), f32(PX, PY, LANES))
    sums = f32(20, 8, LANES)
    state = call(near_steps, levels + (sums,), "near_steps", 10, smem=(9,), flops=1 << 24, size=1 << 22)(
        own_e, own_h, scaled, permit, *near, ya1, yb1, weights
    )
    scratch = [pltpu.VMEM(v.shape, jnp.float32) for v in levels + (sums,)] + [pltpu.SemaphoreType.DMA((2, 2))]
    outs = (f32(3, BX, BY, LANES), f32(3, BX, BY, LANES), f32(n_plane, 1, LANES))
    e_out, h_out, part = call(
        far_steps, outs, "far_steps", 12, scratch=scratch, smem=(11,), hbm_out=(0, 1), flops=1 << 24, size=1 << 22
    )(*state, permit, *far, corner, yb2, ya2, weights)
    both = ("gx", "gy")
    part = lax.all_to_all(part, both, 0, 0, axis_index_groups=planes, tiled=True)
    part = call(add_up, f32(n_column, 1, LANES), "add_up", 1, size=1 << 14)(part)
    part = lax.all_to_all(part, both, 0, 0, axis_index_groups=columns, tiled=True)
    cells = float(BX * n_gx * BY * n_gy * NZ)

    def last(in_ref, out_ref):
        finish(cells, in_ref, out_ref)

    gram = call(last, f32(8, 8), "finish", 1, size=1 << 14)(part)
    return e_out, h_out, gram


def solution(mesh):
    in_specs = (P(None, "gx", "gy", None), P(None, "gx", "gy", None), P("gx", "gy", None), P(), P())
    out_specs = (P(None, "gx", "gy", None), P(None, "gx", "gy", None), P())
    return jax.shard_map(body, mesh=mesh, in_specs=in_specs, out_specs=out_specs, check_vma=False)
```

```python
import jax
import jax.numpy as jnp
from jax import lax
from jax.experimental import pallas as pl
from jax.experimental.pallas import tpu as pltpu
from jax.sharding import PartitionSpec as P

NZ = 64
SOURCES = 2
FILTERS = 4
MATERIALS = 4
ITERS = 4
TIME_STEP = 0.5

BX, BY, LANES = 8, 16, NZ * SOURCES
HALO = ITERS
PX = BX + 2 * HALO
PY = BY + 2 * HALO
XTILES = 49

VMEM = pl.BlockSpec(memory_space=pltpu.VMEM)
HBM = pl.BlockSpec(memory_space=pltpu.HBM)
SMEM = pl.BlockSpec(memory_space=pltpu.SMEM)
PARAMS = pltpu.CompilerParams(vmem_limit_bytes=32 * 1024 * 1024)


def iota(shape, dim):
    return lax.broadcasted_iota(jnp.int32, shape, dim)


def call(kernel, outs, name, n_in, scratch=(), smem=(), hbm=(), hbm_out=(), flops=0, size=0):
    out_specs = tuple(HBM if i in hbm_out else VMEM for i in range(len(outs))) if isinstance(outs, tuple) else VMEM
    return pl.pallas_call(
        kernel,
        out_shape=outs,
        in_specs=[SMEM if i in smem else HBM if i in hbm else VMEM for i in range(n_in)],
        out_specs=out_specs,
        scratch_shapes=list(scratch),
        compiler_params=PARAMS,
        cost_estimate=pl.CostEstimate(flops=flops, bytes_accessed=size, transcendentals=0),
        name=name,
    )


def f32(*shape):
    return jax.ShapeDtypeStruct(shape, jnp.float32)


def x_parts(e, h, wide, narrow):
    return ((e, 0, 4, wide), (e, 1, 4, wide), (e, 2, 4, wide), (h, 0, 3, narrow), (h, 1, 4, wide), (h, 2, 4, wide))


def pack_x(e_ref, h_ref, m_ref, p_ref, f_ref, a_ref, b_ref, own_e, own_h, own_m, table_ref, edge, table, freqs, sems):
    even = lax.rem(lax.axis_index("gx"), 2) == 0
    copies = []
    for side, (out, upper) in enumerate(((a_ref, even), (b_ref, jnp.logical_not(even)))):
        wide = jnp.where(upper, BX - HALO, 0)
        narrow = jnp.where(upper, BX - HALO + 1, 0)
        copies.append(pltpu.make_async_copy(m_ref.at[pl.ds(narrow, 3)], edge.at[side], sems.at[side, 6]))
        row = 0
        for i, (ref, c, n, start) in enumerate(x_parts(e_ref, h_ref, wide, narrow)):
            src = ref.at[c, pl.ds(pl.multiple_of(start * BY, BY), n * BY)]
            copies.append(pltpu.make_async_copy(src, out.at[pl.ds(row, n * BY)], sems.at[side, i]))
            row += n * BY
    for i, (src, dst) in enumerate(((p_ref, table), (f_ref, freqs), (m_ref, own_m), (e_ref, own_e), (h_ref, own_h))):
        copies.append(pltpu.make_async_copy(src, dst, sems.at[2, i]))
    for copy in copies:
        copy.start()
    r, col = iota((NZ, LANES), 0), iota((NZ, LANES), 1)
    low = (col == r).astype(jnp.bfloat16)
    high = (col == r + NZ).astype(jnp.bfloat16)
    for side, out in enumerate((a_ref, b_ref)):
        copies[7 * side].wait()
        for i in range(3):
            cells = edge[side, i].astype(jnp.float32).astype(jnp.bfloat16)
            out[pl.ds(8 * (XTILES - 3 + i), 8)] = jnp.dot(
                cells[:8], low, preferred_element_type=jnp.float32
            ) + jnp.dot(cells[8:], high, preferred_element_type=jnp.float32)
    copies[14].wait()
    copies[15].wait()
    for m in range(MATERIALS):
        table_ref[m] = jnp.full((8, LANES), table[m], jnp.float32)
    for k in range(FILTERS):
        table_ref[MATERIALS + k] = jnp.full((8, LANES), freqs[k], jnp.float32)
    for i, copy in enumerate(copies):
        if i not in (0, 7, 14, 15):
            copy.wait()


def look_up(index, table_ref):
    value = jnp.broadcast_to(table_ref[0, 0:1], index.shape)
    for m in range(1, MATERIALS):
        value = jnp.where(index == float(m), table_ref[m, 0:1], value)
    return value


def spread(rows, offset):
    shape = (rows, LANES)
    return (iota(shape, 1) // SOURCES + offset == iota(shape, 0)).astype(jnp.bfloat16)


def own_cells(m_ref, p_ref, permit_ref, scaled_ref, w_ref):
    row = iota((ITERS * FILTERS, LANES), 0)
    times = (row // FILTERS + 1).astype(jnp.float32) * TIME_STEP
    freqs = jnp.broadcast_to(p_ref[MATERIALS, 0:1], row.shape)
    for k in range(1, FILTERS):
        freqs = jnp.where(row % FILTERS == k, p_ref[MATERIALS + k, 0:1], freqs)
    w_ref[...] = jnp.cos(freqs * times)
    cells = m_ref[...].reshape(BX * BY, NZ).astype(jnp.float32).astype(jnp.bfloat16)
    permit = look_up(jnp.dot(cells, spread(NZ, 0), preferred_element_type=jnp.float32), p_ref)
    permit_ref[...] = permit.reshape(BX, BY, LANES)
    scaled_ref[...] = (TIME_STEP / permit).reshape(BX, BY, LANES)


def fill_ghosts(src, after, p_ref, e_ref, h_ref, s_ref, first_row=0):
    narrow = jnp.where(after, 0, 1)
    row = 0
    for ref, c, n, start in x_parts(e_ref, h_ref, 0, narrow):
        ref[c, pl.ds(start, n)] = src[pl.ds(first_row + row, n * BY)].reshape(n, BY, LANES)
        row += n * BY
    cells = src[pl.ds(first_row + row, 24)].astype(jnp.bfloat16)
    for half in range(2):
        index = jnp.dot(cells, spread(LANES, half * NZ), preferred_element_type=jnp.float32)
        value = TIME_STEP / look_up(index, p_ref)
        for i in range(3):
            s_ref[narrow + i, pl.ds(8 * half, 8)] = value[8 * i : 8 * i + 8]
    unused = jnp.where(after, 3, 0)
    h_ref[0, unused] = jnp.zeros((BY, LANES), jnp.float32)
    s_ref[unused] = jnp.zeros((BY, LANES), jnp.float32)


def edge_rows(ref, low, high):
    first = iota((8, LANES), 0) < HALO
    top = jnp.where(first, pltpu.roll(ref[low, 8:16], HALO, 0), ref[high, 8:16])
    bottom = jnp.where(first, ref[low, 0:8], pltpu.roll(ref[high, 0:8], HALO, 0))
    return top, bottom


def pack_y(parts, ya_ref, yb_ref):
    even = lax.rem(lax.axis_index("gy"), 2) == 0
    for tile, (ref, low, high) in enumerate(parts):
        top, bottom = edge_rows(ref, low, high)
        ya_ref[tile] = jnp.where(even, top, bottom)
        yb_ref[tile] = jnp.where(even, bottom, top)


def unpack_y(parts, ya_ref, yb_ref, other=None):
    even = lax.rem(lax.axis_index("gy"), 2) == 0
    wraps = lax.rem(lax.axis_index("gy") + 1, lax.axis_size("gy")) < 2
    first = iota((8, LANES), 0) < HALO
    for tile, (ref, low, high) in enumerate(parts):
        a, b = ya_ref[tile], yb_ref[tile]
        if other is not None:
            b = jnp.where(wraps, other[tile], b)
        after, before = jnp.where(even, a, b), jnp.where(even, b, a)
        ref[low, BY:PY] = jnp.where(first, after, pltpu.roll(before, HALO, 0))
        ref[high, BY:PY] = jnp.where(first, pltpu.roll(after, HALO, 0), before)


def fields(e, h, s):
    return [e.at[c] for c in range(3)] + [h.at[c] for c in range(3)] + [s]


def pairs_of(refs, planes, base=0):
    return [(ref, base + p, base + p + planes // 2) for ref in refs for p in range(planes // 2)]


def near_side(e_ref, h_ref, s_ref, a_ref, p_ref, ge_ref, gh_ref, gs_ref, ya_ref, yb_ref, corner_ref):
    even = lax.rem(lax.axis_index("gx"), 2) == 0
    other = pl.multiple_of(jnp.where(even, 8 * XTILES, 0), 8)
    fill_ghosts(a_ref, even, p_ref, ge_ref, gh_ref, gs_ref, other)
    own = fields(e_ref, h_ref, s_ref)
    pack_y(pairs_of(own, BX) + pairs_of(fields(ge_ref, gh_ref, gs_ref), HALO), ya_ref, yb_ref)
    start = jnp.where(even, 0, BX - HALO)
    upper = lax.rem(lax.axis_index("gy"), 2) == 1
    for tile, (ref, low, high) in enumerate(pairs_of(own, HALO, start)):
        top, bottom = edge_rows(ref, low, high)
        corner_ref[tile] = jnp.where(upper, top, bottom)


def far_side(b_ref, p_ref, ge_ref, gh_ref, gs_ref, ya_ref, yb_ref):
    odd = lax.rem(lax.axis_index("gx"), 2) == 1
    fill_ghosts(b_ref, odd, p_ref, ge_ref, gh_ref, gs_ref)
    pack_y(pairs_of(fields(ge_ref, gh_ref, gs_ref), HALO), ya_ref, yb_ref)


def up_z(v):
    return jnp.where(iota(v.shape, 1) < LANES - SOURCES, pltpu.roll(v, LANES - SOURCES, 1), 0.0)


def down_z(v):
    return jnp.where(iota(v.shape, 1) >= SOURCES, pltpu.roll(v, SOURCES, 1), 0.0)


def next_y(v):
    return pltpu.roll(v, PY - 1, 0)


def prev_y(v):
    return pltpu.roll(v, 1, 0)


def advance(h_planes, e_planes, e_at, h_at, scale_at, put_e, put_h):
    fresh = {}

    def new_h(c, i):
        return fresh[i][c] if i in fresh else h_at(c, i)

    for i in sorted({*h_planes, *e_planes}):
        e_x, e_y, e_z = (e_at(c, i) for c in range(3))
        if i in h_planes:
            e_yn, e_zn = e_at(1, i + 1), e_at(2, i + 1)
            h_x = h_at(0, i) - TIME_STEP * ((next_y(e_z) - e_z) - (up_z(e_y) - e_y))
            h_y = h_at(1, i) - TIME_STEP * ((up_z(e_x) - e_x) - (e_zn - e_z))
            h_z = h_at(2, i) - TIME_STEP * ((e_yn - e_y) - (next_y(e_x) - e_x))
            fresh[i] = (h_x, h_y, h_z)
            put_h(i, fresh[i])
        if i in e_planes:
            h_x, h_y, h_z = (new_h(c, i) for c in range(3))
            h_yb, h_zb = new_h(1, i - 1), new_h(2, i - 1)
            s = scale_at(i)
            e_x = e_x + s * ((h_z - prev_y(h_z)) - (h_y - down_z(h_y)))
            e_y = e_y + s * ((h_x - down_z(h_x)) - (h_z - h_zb))
            e_z = e_z + s * ((h_y - h_yb) - (h_x - prev_y(h_x)))
            put_e(i, (e_x, e_y, e_z))


def gram_terms(e_at, permit_ref, w_ref, planes, sums):
    even_lane = iota((BY, LANES), 1) % 2 == 0
    w = [jnp.broadcast_to(w_ref[i : i + 1], (BY, LANES)) for i in range(ITERS * FILTERS)]
    for i in planes:
        permit = permit_ref[i]
        for c in range(3):
            e = [e_at(n, c, i)[:BY] for n in range(1, ITERS + 1)]
            f = [sum(w[n * FILTERS + k] * e[n] for n in range(ITERS)) for k in range(FILTERS)]
            g = [v * permit for v in f]
            o = [jnp.where(even_lane, pltpu.roll(v, LANES - 1, 1), pltpu.roll(v, 1, 1)) for v in g]
            at = 0
            sums = list(sums)
            for right in (g, o):
                for k in range(FILTERS):
                    for l in range(k, FILTERS):
                        v = f[k] * right[l]
                        sums[at] = sums[at] + (v[:8] + v[8:])
                        at += 1
    return sums


def both_sides(act):
    even = lax.rem(lax.axis_index("gx"), 2) == 0
    pl.when(even)(lambda: act(True))
    pl.when(jnp.logical_not(even))(lambda: act(False))


def near_h(before, n):
    return range(n - 1, BX + HALO - n) if before else range(n - 1 - HALO, BX - n)


def near_e(before, n):
    if n == 0:
        return range(0, BX + HALO) if before else range(-HALO, BX)
    return range(n, BX + HALO - n) if before else range(n - HALO, BX - n)


def near_planes(before):
    near = range(HALO, BX) if before else range(0, BX - HALO)
    return near, [i for i in range(BX) if i not in near]


def near_steps(own_e, own_h, own_s, permit_ref, ge, gh, gs, ya1, yb1, w_ref, ee, hh, ss, sums_ref):
    def act(before):
        base = BX if before else BX + HALO
        extended = fields(ee.at[0], hh, ss)
        for dst, own, ghost in zip(extended, fields(own_e, own_h, own_s), fields(ge, gh, gs)):
            dst[:BX, :BY] = own[...]
            dst[base : base + HALO, :BY] = ghost[...]
        unpack_y(pairs_of(extended, BX) + pairs_of(extended, HALO, base), ya1, yb1)

        def put_h(i, values):
            for c in range(3):
                hh[c, i % PX] = values[c]

        for n in range(1, ITERS + 1):

            def put_e(i, values, n=n):
                for c in range(3):
                    ee[n, c, i % PX] = values[c]

            advance(
                near_h(before, n), near_e(before, n),
                lambda c, i: ee[n - 1, c, i % PX], lambda c, i: hh[c, i % PX], lambda i: ss[i % PX], put_e, put_h,
            )
        sums = gram_terms(
            lambda n, c, i: ee[n, c, i], permit_ref, w_ref, near_planes(before)[0], [jnp.zeros((8, LANES), jnp.float32)] * 20
        )
        for i in range(20):
            sums_ref[i] = sums[i]

    both_sides(act)


def far_steps(
    ee, hh, ss, sums_in, permit_ref, ge, gh, gs, corner, yb2, ya2, w_ref, e_out, h_out, part_ref, fe, fh, fs, sums_ref, sems
):
    def act(before):
        base = BX + HALO if before else BX
        near, rest = near_planes(before)
        near_h_out = [i for i in range(BX) if i in near_h(before, ITERS)]
        rest_h_out = [i for i in range(BX) if i not in near_h_out]

        def copies_of(which, e, h, e_planes, h_planes):
            e_at, h_at = pl.ds(e_planes[0], len(e_planes)), pl.ds(h_planes[0], len(h_planes))
            return [
                pltpu.make_async_copy(e.at[ITERS, :, e_at, pl.ds(0, BY)], e_out.at[:, e_at], sems.at[which, 0]),
                pltpu.make_async_copy(h.at[:, h_at, pl.ds(0, BY)], h_out.at[:, h_at], sems.at[which, 1]),
            ]

        copies = copies_of(0, ee, hh, near, near_h_out)
        for copy in copies:
            copy.start()
        extended = fields(fe.at[0], fh, fs)
        for dst, ghost in zip(extended, fields(ge, gh, gs)):
            dst[base : base + HALO, :BY] = ghost[...]
        unpack_y(pairs_of(extended, HALO, base), ya2, yb2, corner)
        done = set()
        far = range(-HALO, 0) if before else range(BX, BX + HALO)

        def e_at(n, c, i):
            return (ee if i in near_e(before, n) else fe)[n, c, i % PX]

        def h_at(c, i):
            return (fh if i in done or i in far else hh)[c, i % PX]

        def scale_at(i):
            return (fs if i in far else ss)[i % PX]

        def put_h(i, values):
            done.add(i)
            for c in range(3):
                fh[c, i % PX] = values[c]

        for n in range(1, ITERS + 1):

            def put_e(i, values, n=n):
                for c in range(3):
                    fe[n, c, i % PX] = values[c]

            all_h = range(n - 1 - HALO, BX + HALO - n)
            all_e = range(n - HALO, BX + HALO - n)
            advance(
                [i for i in all_h if i not in near_h(before, n)], [i for i in all_e if i not in near_e(before, n)],
                lambda c, i: e_at(n - 1, c, i), h_at, scale_at, put_e, put_h,
            )
        last = copies_of(1, fe, fh, rest, rest_h_out)
        for copy in last:
            copy.start()
        sums = gram_terms(e_at, permit_ref, w_ref, rest, [sums_in[i] for i in range(20)])
        for i in range(20):
            sums_ref[i] = sums[i]
        for copy in copies + last:
            copy.wait()

    both_sides(act)
    row_of = iota((32, LANES), 0)
    rows = jnp.zeros((32, LANES), jnp.float32)
    at = 0
    for cross in range(2):
        for k in range(FILTERS):
            for l in range(k, FILTERS):
                line = jnp.sum(sums_ref[at], axis=0, keepdims=True)
                rows = jnp.where(row_of == cross * 16 + k * 4 + l, line, rows)
                at += 1

    def entry(shape):
        j = iota(shape, 1)
        k, s, l, t = (j >> 4) & 3, (j >> 3) & 1, (j >> 1) & 3, j & 1
        source = jnp.where(k <= l, s, t)
        which = jnp.where(s == t, 0, 16) + jnp.minimum(k, l) * 4 + jnp.maximum(k, l)
        return jnp.where(j < 64, which, -1), source

    lane_source = (iota((LANES, LANES), 0) & 1 == entry((LANES, LANES))[1]).astype(jnp.float32)
    totals = jnp.dot(rows, lane_source, precision=lax.Precision.HIGHEST, preferred_element_type=jnp.float32)
    vector = jnp.sum(jnp.where(row_of == entry((32, LANES))[0], totals, 0.0), axis=0, keepdims=True)
    part_ref[...] = jnp.broadcast_to(vector[None], part_ref.shape)


def add_up(in_ref, out_ref):
    out_ref[...] = jnp.broadcast_to(jnp.sum(in_ref[...], axis=0, keepdims=True), out_ref.shape)


def finish(cells, in_ref, out_ref):
    vector = jnp.broadcast_to(jnp.sum(in_ref[...], axis=0), (8, LANES))
    picked = jnp.where(iota((8, LANES), 1) // 8 == iota((8, LANES), 0), vector, 0.0)
    fold = (iota((LANES, LANES), 0) % 8 == iota((LANES, LANES), 1)).astype(jnp.float32)
    total = jnp.dot(picked, fold, precision=lax.Precision.HIGHEST, preferred_element_type=jnp.float32)
    out_ref[...] = total[:, :8] / cells


def swap_pairs(count, odd, wrap=True):
    if not odd:
        return [(i, i ^ 1) for i in range(count)]
    inner = range(count) if wrap else range(1, count - 1)
    return [(i, (i + 1) % count if i % 2 else (i - 1) % count) for i in inner]


def sum_groups(n_gx, n_gy):
    planes, columns = {}, {}
    for gx in range(n_gx):
        for gy in range(n_gy):
            y, z_high, x = gx // 8, (gx // 4) % 2, gx % 4
            z, core = z_high * 8 + gy // 2, gy % 2
            planes.setdefault(z, []).append(gx * n_gy + gy)
            columns.setdefault((x, y, core), []).append(gx * n_gy + gy)
    return list(planes.values()), list(columns.values())


def body(e_field, h_field, material, permittivity, frequencies):
    n_gx, n_gy = lax.axis_size("gx"), lax.axis_size("gy")
    x_message = (f32(XTILES * 8, LANES),) * 2
    y_first = (f32(7 * (BX + HALO) // 2, 8, LANES),) * 2
    y_corner = f32(7 * HALO // 2, 8, LANES)
    scratch = (pltpu.VMEM((2, 3, BY, NZ), jnp.int32), pltpu.SMEM((MATERIALS,), jnp.float32), pltpu.SMEM((FILTERS,), jnp.float32), pltpu.SemaphoreType.DMA((3, 7)))
    block = [
        pltpu.with_memory_space_constraint(v, pltpu.HBM)
        for v in (e_field.reshape(3, BX * BY, LANES), h_field.reshape(3, BX * BY, LANES), material, permittivity, frequencies)
    ]
    outs = x_message + (f32(3, BX * BY, LANES), f32(3, BX * BY, LANES), jax.ShapeDtypeStruct((BX, BY, NZ), jnp.int32))
    outs += (f32(MATERIALS + FILTERS, 8, LANES),)
    send_a, send_b, own_e, own_h, own_m, table = call(
        pack_x, outs, "pack_x", 5, scratch=scratch, hbm=(0, 1, 2, 3, 4), size=1 << 20
    )(*block)
    own_e, own_h = own_e.reshape(e_field.shape), own_h.reshape(h_field.shape)
    near_pairs = [[i, i + 1] for i in range(0, n_gx, 2)]
    got_a = lax.all_gather(send_a, "gx", axis_index_groups=near_pairs, tiled=True)
    got_b = lax.ppermute(send_b, "gx", swap_pairs(n_gx, True))
    outs = (f32(BX, BY, LANES), f32(BX, BY, LANES), f32(ITERS * FILTERS, LANES))
    permit, scaled, weights = call(own_cells, outs, "own_cells", 2, size=1 << 18)(own_m, table)
    ghosts = (f32(3, HALO, BY, LANES), f32(3, HALO, BY, LANES), f32(HALO, BY, LANES))
    *near, send_a, send_b, send_c = call(near_side, ghosts + y_first + (y_corner,), "near_side", 5, size=1 << 20)(
        own_e, own_h, scaled, got_a, table
    )
    end = n_gy - 1
    diagonal = [(a * n_gy + g, b * n_gy + end - g) for a, b in swap_pairs(n_gx, True) for g in (0, end)]
    yb1 = lax.ppermute(send_b, "gy", swap_pairs(n_gy, True))
    corner = lax.ppermute(send_c, ("gx", "gy"), diagonal)
    ya1 = lax.ppermute(send_a, "gy", swap_pairs(n_gy, False))
    got_b, ya1 = lax.optimization_barrier((got_b, ya1))
    *far, send_a, send_b = call(far_side, ghosts + (y_corner, y_corner), "far_side", 2, size=1 << 20)(
        got_b, table
    )
    ya2 = lax.ppermute(send_a, "gy", swap_pairs(n_gy, False))
    yb2 = lax.ppermute(send_b, "gy", swap_pairs(n_gy, True, wrap=False))
    planes, columns = sum_groups(n_gx, n_gy)
    n_plane, n_column = len(planes[0]), len(columns[0])
    levels = (f32(ITERS + 1, 3, PX, PY, LANES), f32(3, PX, PY, LANES), f32(PX, PY, LANES))
    sums = f32(20, 8, LANES)
    state = call(near_steps, levels + (sums,), "near_steps", 10, flops=1 << 24, size=1 << 22)(
        own_e, own_h, scaled, permit, *near, ya1, yb1, weights
    )
    scratch = [pltpu.VMEM(v.shape, jnp.float32) for v in levels + (sums,)] + [pltpu.SemaphoreType.DMA((2, 2))]
    outs = (f32(3, BX, BY, LANES), f32(3, BX, BY, LANES), f32(n_plane, 1, LANES))
    e_out, h_out, part = call(
        far_steps, outs, "far_steps", 12, scratch=scratch, hbm_out=(0, 1), flops=1 << 24, size=1 << 22
    )(*state, permit, *far, corner, yb2, ya2, weights)
    both = ("gx", "gy")
    part = lax.all_to_all(part, both, 0, 0, axis_index_groups=planes, tiled=True)
    part = call(add_up, f32(n_column, 1, LANES), "add_up", 1, size=1 << 14)(part)
    part = lax.all_to_all(part, both, 0, 0, axis_index_groups=columns, tiled=True)
    cells = float(BX * n_gx * BY * n_gy * NZ)

    def last(in_ref, out_ref):
        finish(cells, in_ref, out_ref)

    gram = call(last, f32(8, 8), "finish", 1, size=1 << 14)(part)
    return e_out, h_out, gram


def solution(mesh):
    in_specs = (P(None, "gx", "gy", None), P(None, "gx", "gy", None), P("gx", "gy", None), P(), P())
    out_specs = (P(None, "gx", "gy", None), P(None, "gx", "gy", None), P())
    return jax.shard_map(body, mesh=mesh, in_specs=in_specs, out_specs=out_specs, check_vma=False)
```
